512 devices in a mesh: row: 16 (over x_lo, y), col: 32 (over x_hi, z, core).
Axes of the slice: x: 4 (x_hi: 2, x_lo: 2; x = x_hi * 2 + x_lo), y: 8, z: 8, core: 2. Of those that a mesh axis runs over, the one named last changes fastest.
Arguments:
- matrix: float32 [4096, 8192], P('row', 'col'), may hold values from -64 to 64
- right_factor: float32 [8192, 8192], P('row', 'col'), may hold values from -6 to 6
Outputs:
- rotated_matrix: float32 [4096, 8192], P('row', 'col')
- rotated_factor: float32 [8192, 8192], P('row', 'col')
The draws below stay inside these ranges and needn't reach their ends.
All inputs are finite; a program needn't handle non-finite values.
Results may differ from the reference program's by a relative error of at most 0.0003.
Values sent between devices are 32-bit elements; how exact they have to be, the bound alone decides.
A program may use at most 64 MiB of HBM per device.

```python
import math
import jax
import jax.numpy as jnp
import numpy as np
from jax import lax

BLK = 128
ROUNDS = 6
STEPS = 2
M = 4096
N = 8192


def draw_matrix(key, part):
    key = jax.random.fold_in(key, 11)
    keys = jax.random.split(key, 3)
    ramp = 1.0 + 0.75 * jnp.arange(M, dtype=jnp.float32)[:, None] / M
    row_scale = jnp.exp(jax.random.uniform(keys[0], (M, 1), jnp.float32, math.log(0.3), math.log(3.0))) * ramp
    col_scale = jnp.exp(jax.random.uniform(keys[1], (1, N), jnp.float32, math.log(0.3), math.log(3.0)))
    entries = jax.random.truncated_normal(keys[2], -4.0, 4.0, (M, N), jnp.float32)
    return (entries * row_scale * col_scale).astype(jnp.float32)


def block_levels(own_key, dims, shards, low, high):
    gain, own = 1.0, jax.random.fold_in(own_key, 6)
    for axis_at, parts in shards:
        draws = jnp.exp(jax.random.uniform(jax.random.fold_in(own, axis_at), (parts,), jnp.float32, low / len(shards), high / len(shards)))
        gain = gain * jnp.repeat(draws, dims[axis_at] // parts).reshape([-1 if axis == axis_at else 1 for axis in range(len(dims))])
    return gain


def gaussian(rng, dims, width, most, cuts=(), kind=jnp.bfloat16):
    loudness = block_levels(rng, dims, cuts, -0.22, 0.18) if cuts else 1.0
    array = jax.random.normal(rng, dims, jnp.float32) * width * loudness
    return jnp.minimum(jnp.maximum(array, -most), most).astype(kind)


def setup_inputs(seed: int = 0) -> dict:
    arg_keys = jax.random.split(jax.random.key(seed), 3)
    matrix = draw_matrix(jax.random.fold_in(arg_keys[2], 71), 0)
    right_factor = gaussian(arg_keys[1], (N, N), 1.0, 6.0, ((0, 16), (1, 32)), jnp.float32)
    return {"matrix": matrix, "right_factor": right_factor}


def gram_of(block):
    return lax.dot_general(block, block, (((0,), (0,)), ((), ())), precision=lax.Precision.HIGHEST, preferred_element_type=jnp.float32)


def times_rotation(block, rotation):
    return jnp.dot(block, rotation, precision=lax.Precision.HIGHEST, preferred_element_type=jnp.float32)


def permute(values, round_index, axis):
    order = values.shape[axis]
    last_index = order - 1
    head = lax.slice_in_dim(values, 0, last_index, axis=axis)
    moved = jnp.roll(jnp.flip(head, axis), (2 * round_index - order + 2) % last_index, axis)
    before = lax.slice_in_dim(moved, 0, round_index, axis=axis)
    after = lax.slice_in_dim(moved, round_index + 1, last_index, axis=axis)
    fixed = lax.slice_in_dim(values, last_index, order, axis=axis)
    tail = lax.slice_in_dim(values, round_index, round_index + 1, axis=axis)
    return jnp.concatenate([before, fixed, after, tail], axis=axis)


def rotation_round(round_index, gram_pair, rotation):
    order = gram_pair.shape[0]
    indices = np.arange(order)
    last_index = order - 1
    partner = np.where(indices == last_index, round_index, np.where(indices == round_index, last_index, np.mod(2 * round_index - indices, last_index)))
    lower_side = jnp.asarray(indices < partner)
    diagonal = jnp.diagonal(gram_pair)
    columns = permute(gram_pair, round_index, 1)
    across = jnp.diagonal(columns)
    spread = permute(diagonal, round_index, 0) - diagonal
    sign_of = jnp.where(spread >= 0, 1.0, -1.0).astype(gram_pair.dtype)
    half_angle = 0.5 * sign_of * jnp.arctan2(2.0 * across, jnp.abs(spread))
    angle = jnp.where(lower_side, half_angle, permute(half_angle, round_index, 0))
    cosine = jnp.cos(angle)
    sine = jnp.sin(angle)
    signed = jnp.where(lower_side, -sine, sine)
    mixed = gram_pair * cosine[None, :] + columns * signed[None, :]
    gram_pair = mixed * cosine[:, None] + permute(mixed, round_index, 0) * signed[:, None]
    rotation = rotation * cosine[None, :] + permute(rotation, round_index, 1) * signed[None, :]
    return gram_pair, rotation


def inner_solve(gram_pair):
    rotation = jnp.eye(gram_pair.shape[0], dtype=gram_pair.dtype)
    for round_index in range(ROUNDS):
        gram_pair, rotation = rotation_round(round_index, gram_pair, rotation)
    return gram_pair, rotation


def advance(pairs):
    upper = pairs[:, :, :BLK]
    lower = pairs[:, :, BLK:]
    new_upper = jnp.concatenate([upper[:1], lower[:1], upper[1:-1]], axis=0)
    new_lower = jnp.concatenate([lower[1:], upper[-1:]], axis=0)
    return jnp.concatenate([new_upper, new_lower], axis=2)


def one_pair(operands):
    slab_pair, factor_pair = operands
    rotated_gram, rotation = inner_solve(gram_of(slab_pair))
    return times_rotation(slab_pair, rotation), times_rotation(factor_pair, rotation)


def reference(matrix, right_factor):
    pair_count = N // (2 * BLK)
    slab_pairs = matrix.reshape(M, pair_count, 2 * BLK).transpose(1, 0, 2)
    factor_pairs = right_factor.reshape(N, pair_count, 2 * BLK).transpose(1, 0, 2)
    for section in range(STEPS):
        slab_pairs, factor_pairs = lax.map(one_pair, (slab_pairs, factor_pairs))
        slab_pairs = advance(slab_pairs)
        factor_pairs = advance(factor_pairs)
    rotated_matrix = slab_pairs.transpose(1, 0, 2).reshape(M, N)
    rotated_factor = factor_pairs.transpose(1, 0, 2).reshape(N, N)
    return rotated_matrix, rotated_factor
```

```python
import jax
import jax.numpy as jnp
from jax import lax
from jax.experimental import pallas as pl
from jax.experimental.pallas import tpu as pltpu
from jax.sharding import PartitionSpec as P

BLK = 128
ROUNDS = 6
ROWS = 8
KEPT = 6
MESH = pl.DeviceIdType.MESH
F32 = jnp.float32


def iota(shape, axis):
    return lax.broadcasted_iota(jnp.int32, shape, axis)


def next_lane(x):
    return pltpu.roll(x, BLK - 1, 1)


def previous_lane(x):
    return pltpu.roll(x, 1, 1)


def below(x, n):
    even, odd = x
    up_even, up_odd = pltpu.roll(even, ROWS - 1, 0), pltpu.roll(odd, ROWS - 1, 0)
    return (odd, up_even) if n == 1 else (up_even, up_odd)


def above(x, n):
    even, odd = x
    down_even, down_odd = pltpu.roll(even, 1, 0), pltpu.roll(odd, 1, 0)
    return (down_odd, even) if n == 1 else (down_even, down_odd)


def both(function, *operands):
    return tuple(function(*parts) for parts in zip(*operands))


def lanes(x, index):
    return jnp.take_along_axis(x, jnp.broadcast_to(index, x.shape), axis=1)


def halves(x):
    high = x.astype(jnp.bfloat16)
    return high, (x - high.astype(F32)).astype(jnp.bfloat16)


def dot(x, y):
    return jnp.dot(x, y, preferred_element_type=F32)


def times(x, split):
    x_high, x_low = halves(x)
    high, low = split
    return dot(x_high, high) + (dot(x_low, high) + dot(x_high, low))


def backwards(x):
    return lanes(x, BLK - 1 - iota((1, BLK), 1))


def diagonals(x, place):
    place[...] = pltpu.roll(x, 1, 1, stride=1, stride_axis=0).T[:2 * ROWS]
    return place[pl.ds(0, ROWS, stride=2)], place[pl.ds(1, ROWS, stride=2)]


def flipped_rows(x):
    index = jnp.clip(KEPT - 1 - iota(x.shape, 0), 0, ROWS - 1)
    return jnp.take_along_axis(x, index, axis=0)


def pack(even, odd):
    j, lane = iota((ROWS, BLK), 0), iota((ROWS, BLK), 1)
    odd = flipped_rows(odd)
    high = pltpu.roll(odd, 0, 1, stride=1, stride_axis=0)
    low = pltpu.roll(pltpu.roll(odd, 0, 1, stride=3, stride_axis=0), BLK - 11, 1)
    return jnp.where(lane < j, high, jnp.where(lane < 2 * j, low, even))[:KEPT]


def unpack(packed):
    i, lane = iota((ROWS, BLK), 0), iota((ROWS, BLK), 1)
    back = flipped_rows(packed)
    high = pltpu.roll(pltpu.roll(back, 0, 1, stride=1, stride_axis=0), BLK - 5, 1)
    low = pltpu.roll(pltpu.roll(back, 0, 1, stride=3, stride_axis=0), BLK - 4, 1)
    return packed, jnp.where(lane >= BLK - 5 + i, high, low)


def gram_bands(upper, lower, place):
    left = jnp.concatenate([upper, backwards(lower)], axis=1)
    right = jnp.concatenate([backwards(upper), lower], axis=1)
    gram = lax.dot_general(
        left, right, (((0,), (0,)), ((), ())), precision=lax.Precision.HIGHEST, preferred_element_type=F32
    )
    blocks = (gram[:BLK, :BLK], gram[:BLK, BLK:], gram[BLK:, :BLK], gram[BLK:, BLK:])
    return [pack(*diagonals(block, place.at[at])) for at, block in enumerate(blocks)]


def angles(round_index, uu, uv, vv):
    lane = iota((1, BLK), 1)
    spread = vv[0][0:1] - uu[0][0:1]
    across = 2.0 * uv[0][0:1]
    width = jnp.abs(spread)
    scale = jnp.maximum(jnp.abs(across), width)
    live = scale > 0
    inverse = 1.0 / jnp.where(live, scale, 1.0)
    across = across * inverse
    width = jnp.where(live, width * inverse, 1.0)
    root = lax.rsqrt(across * across + width * width)
    square = 0.5 + 0.5 * width * root
    root_cosine = lax.rsqrt(square)
    cosine = square * root_cosine
    sine = 0.5 * across * root * root_cosine
    upper_first = (lane == 0) | (lane > round_index)
    positive = (spread > 0) | ((spread == 0) & upper_first)
    return cosine, jnp.where(positive, sine, -sine)


def shift_pairs(uu, uv, vu, vv):
    lane, row = iota((ROWS, BLK), 1), iota((ROWS, BLK), 0)
    last, first, second = lane == BLK - 1, lane == 0, lane == 1
    uu_next, uv_next = both(next_lane, uu), both(next_lane, uv)
    uu_back, uv_back, vu_back, vv_back = (both(previous_lane, x) for x in (uu, uv, vu, vv))
    vu_1, vv_b1, uv_n1 = above(vu, 1), below(vv, 1), below(uv_next, 1)
    uu_n2, uv_n2, vu_b2, vv_b1up = below(uu_next, 2), below(uv_next, 2), above(vu_back, 2), above(vv_back, 1)
    uv_b1up = above(uv_back, 1)
    out = []
    for at in range(2):
        q = 2 * row + at
        new_uu = jnp.where(last, vu_1[at] if at else jnp.where(q == 0, vv[at], vu_1[at]), uu_next[at])
        new_uv = jnp.where(q == lane - 1, uu_n2[at], uv_n2[at])
        new_uv = jnp.where(q == lane, uv_n1[at], new_uv)
        new_uv = jnp.where(last, vv_b1[at], new_uv)
        if at:
            new_vu = jnp.where(q == 1, jnp.where(second, uu[at], uv[at]), vu_b2[at])
        else:
            new_vu = jnp.where(q == 0, new_uv, vu_b2[at])
        new_vv = jnp.where(q == lane - 1, vu_back[at], vv_back[at])
        new_vv = jnp.where(q == lane, vv_b1up[at], new_vv)
        new_vv = jnp.where(first, vv[at], new_vv)
        new_vv = jnp.where(second & (q == at), uv_b1up[at] if at else uu_back[at], new_vv)
        out.append((new_uu, new_uv, new_vu, new_vv))
    return tuple(zip(*out))


def solve(uu, uv, vu, vv):
    tall = (2 * BLK, BLK)
    row, lane = iota(tall, 0), iota(tall, 1)
    q_u = jnp.where(row == lane, 1.0, 0.0).astype(F32)
    q_v = jnp.where(row == 2 * BLK - 1 - lane, 1.0, 0.0).astype(F32)
    for round_index in range(ROUNDS):
        cos, sin = angles(round_index, uu, uv, vv)
        q_u, q_v = q_u * cos - q_v * sin, q_u * sin + q_v * cos
        if round_index + 1 == ROUNDS:
            break
        near = [jnp.broadcast_to(x, (ROWS, BLK)) for x in (cos, sin)]
        new = []
        for at in range(2):
            far_cos, far_sin = (pltpu.roll(x, at, 1, stride=2, stride_axis=0) for x in near)
            a, b, c, d = uu[at], uv[at], vu[at], vv[at]
            a, b = a * far_cos - b * far_sin, a * far_sin + b * far_cos
            c, d = c * far_cos - d * far_sin, c * far_sin + d * far_cos
            a, c = a * cos - c * sin, a * sin + c * cos
            b, d = b * cos - d * sin, b * sin + d * cos
            new.append((a, b, c, d))
        uu, uv, vu, vv = shift_pairs(*zip(*new))
        q_u, q_v = (
            jnp.where(lane == BLK - 1, q_v, next_lane(q_u)),
            jnp.where(lane == 0, q_v, jnp.where(lane == 1, previous_lane(q_u), previous_lane(q_v))),
        )
    return q_u, q_v


def block_columns(q_u, q_v, lower):
    last_round = ROUNDS - 1
    lane = iota((1, BLK), 1)
    upper_index = jnp.where(lane >= last_round, lane - last_round, last_round - lane)
    from_u = jnp.where(lane < last_round, BLK - last_round + lane, 0)
    from_v = jnp.where(lane == BLK - 1, 0, BLK - 1 + last_round - lane)
    lower_index = jnp.where(lane < last_round, from_u, from_v)
    index = jnp.where(lower, lower_index, upper_index)
    first = lane < last_round
    in_u = (first & lower) | (jnp.logical_not(first) & jnp.logical_not(lower))
    return jnp.where(in_u, lanes(q_u, index), lanes(q_v, index))


def kernel(
    rows, pairs,
    s_in, f_in, s_out, f_out,
    s_own, f_own, s_half, f_half, s_pair, f_pair, s_done, f_done, bands, place, total,
    load_sem, store_sem, sum_send, sum_recv, move_send, move_recv,
):
    row, col = lax.axis_index("row"), lax.axis_index("col")
    last = pairs - 1

    load_s = pltpu.make_async_copy(s_in, s_own, load_sem.at[0])
    load_f = pltpu.make_async_copy(f_in, f_own, load_sem.at[1])
    load_s.start()
    load_f.start()

    up_to = jnp.where(col == 0, 1, jnp.where(col == last, last - 1, jnp.where(col == last - 1, last, col + 2)))
    up_pair = jnp.where(col >= last - 1, 1, 0)
    up_half = jnp.where(col == last, 1, 0)
    low_to = jnp.where(col == 0, 2, jnp.where(col == 1, 0, col - 2))
    low_pair = jnp.where(col <= 1, 0, 1)
    low_half = jnp.where(col == 0, 0, 1)
    stays_a = jnp.where(col == 0, 0, 1)
    stays_b = jnp.where(col == 0, 1, 0)
    half_b = jnp.where(col == last, 1, 0)

    barrier = pltpu.get_barrier_semaphore()
    peers = [lax.rem(row + rows // 2 * (d % 2) + d // 2, rows) for d in range(rows - 1, 0, -1)]
    for peer in peers:
        pl.semaphore_signal(barrier, inc=1, device_id={"row": peer}, device_id_type=MESH)
    for partner in (up_to, low_to):
        pl.semaphore_signal(barrier, inc=1, device_id={"col": partner}, device_id_type=MESH)

    def send(at, source, target, peer):
        return pltpu.make_async_remote_copy(
            src_ref=source, dst_ref=target, send_sem=sum_send.at[at], recv_sem=sum_recv.at[at],
            device_id={"row": peer}, device_id_type=MESH,
        )

    def share(at):
        own = bands.at[at, row]
        for peer in peers:
            send(at, own, own, peer).start()

    def form(at, upper, lower):
        for block, packed in enumerate(gram_bands(upper, lower, place)):
            bands[at, row, KEPT * block:KEPT * (block + 1)] = packed

    def summed(at):
        rest = bands.at[at, pl.ds(0, rows - 1)]
        with jax.named_scope("sum_wait"):
            send(at, rest, rest, peers[0]).wait_recv()
        whole = bands[at, 0]
        for d in range(1, rows):
            whole = whole + bands[at, d]
        total[at, 0:4 * KEPT] = whole
        return [unpack(total[at, KEPT * block:KEPT * block + ROWS]) for block in range(4)]

    total[...] = jnp.zeros(total.shape, F32)
    with jax.named_scope("load_slab"):
        load_s.wait()
    with jax.named_scope("gram_first"):
        form(0, s_own[:, :BLK], s_own[:, BLK:])
    with jax.named_scope("entry"):
        pl.semaphore_wait(barrier, rows + 1)
    share(0)
    blocks = summed(0)
    with jax.named_scope("solve_first"):
        q_u, q_v = solve(*blocks)
        split = [halves(block_columns(q_u, q_v, lower)) for lower in (False, True)]
        split = [jnp.concatenate(parts, axis=1) for parts in zip(*split)]

    def move(kind, half, at, target, pair, half_at, to):
        return pltpu.make_async_remote_copy(
            src_ref=half.at[at], dst_ref=target.at[pair, half_at],
            send_sem=move_send.at[kind, at], recv_sem=move_recv.at[kind, pair],
            device_id={"col": to}, device_id_type=MESH,
        )

    def moves(kind, half, target):
        return (
            move(kind, half, 0, target, up_pair, up_half, up_to),
            move(kind, half, 1, target, low_pair, low_half, low_to),
        )

    def rotate(own, half, target):
        moved = times(own[...], split)
        half[0] = moved[:, :BLK]
        half[1] = moved[:, BLK:]

    def stay(half, target):
        target[0, stays_a] = half[stays_a]
        target[1, half_b] = half[stays_b]

    s_moves, f_moves = moves(0, s_half, s_pair), moves(1, f_half, f_pair)
    with jax.named_scope("apply_slab"):
        rotate(s_own, s_half, s_pair)
    for copy in s_moves:
        copy.start()
    load_f.wait()
    with jax.named_scope("apply_factor"):
        stay(s_half, s_pair)
        rotate(f_own, f_half, f_pair)
        stay(f_half, f_pair)

    def arrived(kind, half, target, pair):
        move(kind, half, 0, target, pair, 0, up_to).wait_recv()

    for pair in range(2):
        with jax.named_scope("slab_arrival"):
            arrived(0, s_half, s_pair, pair)
        with jax.named_scope("gram_second"):
            form(1 + pair, s_pair[pair, 0], s_pair[pair, 1])
        share(1 + pair)
    for copy in f_moves:
        copy.start()

    lower_of = (col == 1, col != last)

    def finish(target, done, pair, split):
        whole = jnp.concatenate([target[pair, 0], target[pair, 1]], axis=1)
        done[:, pair * BLK:(pair + 1) * BLK] = times(whole, split)

    splits = []
    for pair in range(2):
        blocks = summed(1 + pair)
        with jax.named_scope("solve_second"):
            q_u, q_v = solve(*blocks)
            splits.append(halves(block_columns(q_u, q_v, lower_of[pair])))
        with jax.named_scope("finish_slab"):
            finish(s_pair, s_done, pair, splits[pair])
    store_s = pltpu.make_async_copy(s_done, s_out, store_sem.at[0])
    store_s.start()
    for pair in range(2):
        with jax.named_scope("factor_arrival"):
            arrived(1, f_half, f_pair, pair)
        with jax.named_scope("finish_factor"):
            finish(f_pair, f_done, pair, splits[pair])
    store_f = pltpu.make_async_copy(f_done, f_out, store_sem.at[1])
    store_f.start()

    with jax.named_scope("last_waits"):
        for copy in s_moves + f_moves:
            copy.wait_send()
        for at in range(3):
            rest = bands.at[at, pl.ds(0, rows - 1)]
            send(at, rest, rest, peers[0]).wait_send()
        store_s.wait()
        store_f.wait()


def solution(mesh):
    rows, pairs = mesh.shape["row"], mesh.shape["col"]

    def shards(matrix, right_factor):
        s_rows, f_rows = matrix.shape[0], right_factor.shape[0]
        return pl.pallas_call(
            lambda *refs: kernel(rows, pairs, *refs),
            out_shape=(
                jax.ShapeDtypeStruct(matrix.shape, F32),
                jax.ShapeDtypeStruct(right_factor.shape, F32),
            ),
            in_specs=[pl.BlockSpec(memory_space=pl.ANY)] * 2,
            out_specs=[pl.BlockSpec(memory_space=pl.ANY)] * 2,
            scratch_shapes=[
                pltpu.VMEM(matrix.shape, F32),
                pltpu.VMEM(right_factor.shape, F32),
                pltpu.VMEM((2, s_rows, BLK), F32),
                pltpu.VMEM((2, f_rows, BLK), F32),
                pltpu.VMEM((2, 2, s_rows, BLK), F32),
                pltpu.VMEM((2, 2, f_rows, BLK), F32),
                pltpu.VMEM(matrix.shape, F32),
                pltpu.VMEM(right_factor.shape, F32),
                pltpu.VMEM((3, rows, 4 * KEPT, BLK), F32),
                pltpu.VMEM((4, 2 * ROWS, BLK), F32),
                pltpu.VMEM((3, 4 * ROWS, BLK), F32),
                pltpu.SemaphoreType.DMA((2,)),
                pltpu.SemaphoreType.DMA((2,)),
                pltpu.SemaphoreType.DMA((3,)),
                pltpu.SemaphoreType.DMA((3,)),
                pltpu.SemaphoreType.DMA((2, 2)),
                pltpu.SemaphoreType.DMA((2, 2)),
            ],
            compiler_params=pltpu.CompilerParams(collective_id=0, has_side_effects=True),
            name="tournament",
        )(matrix, right_factor)

    spec = P("row", "col")
    return jax.shard_map(shards, mesh=mesh, in_specs=(spec, spec), out_specs=(spec, spec), check_vma=False)
```

```python
import jax
import jax.numpy as jnp
from jax import lax
from jax.experimental import pallas as pl
from jax.experimental.pallas import tpu as pltpu
from jax.sharding import PartitionSpec as P

BLK = 128
ROUNDS = 6
ROWS = 8
KEPT = 6
GRANT = 32 * 1024 * 1024
MESH = pl.DeviceIdType.MESH
F32 = jnp.float32


def iota(shape, axis):
    return lax.broadcasted_iota(jnp.int32, shape, axis)


def next_lane(x):
    return pltpu.roll(x, BLK - 1, 1)


def previous_lane(x):
    return pltpu.roll(x, 1, 1)


def below(x, n):
    even, odd = x
    up_even, up_odd = pltpu.roll(even, ROWS - 1, 0), pltpu.roll(odd, ROWS - 1, 0)
    return (odd, up_even) if n == 1 else (up_even, up_odd)


def above(x, n):
    even, odd = x
    down_even, down_odd = pltpu.roll(even, 1, 0), pltpu.roll(odd, 1, 0)
    return (down_odd, even) if n == 1 else (down_even, down_odd)


def both(function, *operands):
    return tuple(function(*parts) for parts in zip(*operands))


def lanes(x, index):
    return jnp.take_along_axis(x, jnp.broadcast_to(index, x.shape), axis=1)


def halves(x):
    high = x.astype(jnp.bfloat16)
    return high, (x - high.astype(F32)).astype(jnp.bfloat16)


def dot(x, y):
    return jnp.dot(x, y, preferred_element_type=F32)


def times(x_split, split):
    x_high, x_low = x_split
    high, low = split
    return dot(x_high, high) + (dot(x_low, high) + dot(x_high, low))


def products(x, y):
    x_high, x_low = halves(x)
    y_high, y_low = halves(y)

    def columns(a, b):
        return lax.dot_general(a, b, (((0,), (0,)), ((), ())), preferred_element_type=F32)

    small = columns(x_high, y_low) + columns(x_low, y_high)
    return columns(x_high, y_high) + (small + columns(x_low, y_low))


def backwards(x):
    return lanes(x, BLK - 1 - iota((1, BLK), 1))


def diagonals(x, place):
    place[...] = pltpu.roll(x, 1, 1, stride=1, stride_axis=0).T[:2 * ROWS]
    return place[pl.ds(0, ROWS, stride=2)], place[pl.ds(1, ROWS, stride=2)]


def flipped_rows(x):
    index = jnp.clip(KEPT - 1 - iota(x.shape, 0), 0, ROWS - 1)
    return jnp.take_along_axis(x, index, axis=0)


def pack(even, odd):
    j, lane = iota((ROWS, BLK), 0), iota((ROWS, BLK), 1)
    odd = flipped_rows(odd)
    high = pltpu.roll(odd, 0, 1, stride=1, stride_axis=0)
    low = pltpu.roll(pltpu.roll(odd, 0, 1, stride=3, stride_axis=0), BLK - 11, 1)
    return jnp.where(lane < j, high, jnp.where(lane < 2 * j, low, even))[:KEPT]


def unpack(packed):
    i, lane = iota((ROWS, BLK), 0), iota((ROWS, BLK), 1)
    back = flipped_rows(packed)
    high = pltpu.roll(pltpu.roll(back, 0, 1, stride=1, stride_axis=0), BLK - 5, 1)
    low = pltpu.roll(pltpu.roll(back, 0, 1, stride=3, stride_axis=0), BLK - 4, 1)
    return packed, jnp.where(lane >= BLK - 5 + i, high, low)


def gram_bands(upper, lower, place):
    left = jnp.concatenate([upper, backwards(lower)], axis=1)
    right = jnp.concatenate([backwards(upper), lower], axis=1)
    gram = products(left, right)
    blocks = (gram[:BLK, :BLK], gram[:BLK, BLK:], gram[BLK:, :BLK], gram[BLK:, BLK:])
    return [pack(*diagonals(block, place.at[at])) for at, block in enumerate(blocks)]


def angles(round_index, uu, uv, vv):
    lane = iota((1, BLK), 1)
    spread = vv[0][0:1] - uu[0][0:1]
    across = 2.0 * uv[0][0:1]
    width = jnp.abs(spread)
    scale = jnp.maximum(jnp.abs(across), width)
    live = scale > 0
    inverse = 1.0 / jnp.where(live, scale, 1.0)
    across = across * inverse
    width = jnp.where(live, width * inverse, 1.0)
    root = lax.rsqrt(across * across + width * width)
    square = 0.5 + 0.5 * width * root
    root_cosine = lax.rsqrt(square)
    cosine = square * root_cosine
    sine = 0.5 * across * root * root_cosine
    upper_first = (lane == 0) | (lane > round_index)
    positive = (spread > 0) | ((spread == 0) & upper_first)
    return cosine, jnp.where(positive, sine, -sine)


def shift_pairs(uu, uv, vu, vv):
    lane, row = iota((ROWS, BLK), 1), iota((ROWS, BLK), 0)
    last, first, second = lane == BLK - 1, lane == 0, lane == 1
    uu_next, uv_next = both(next_lane, uu), both(next_lane, uv)
    uu_back, uv_back, vu_back, vv_back = (both(previous_lane, x) for x in (uu, uv, vu, vv))
    vu_1, vv_b1, uv_n1 = above(vu, 1), below(vv, 1), below(uv_next, 1)
    uu_n2, uv_n2, vu_b2, vv_b1up = below(uu_next, 2), below(uv_next, 2), above(vu_back, 2), above(vv_back, 1)
    uv_b1up = above(uv_back, 1)
    out = []
    for at in range(2):
        q = 2 * row + at
        new_uu = jnp.where(last, vu_1[at] if at else jnp.where(q == 0, vv[at], vu_1[at]), uu_next[at])
        new_uv = jnp.where(q == lane - 1, uu_n2[at], uv_n2[at])
        new_uv = jnp.where(q == lane, uv_n1[at], new_uv)
        new_uv = jnp.where(last, vv_b1[at], new_uv)
        if at:
            new_vu = jnp.where(q == 1, jnp.where(second, uu[at], uv[at]), vu_b2[at])
        else:
            new_vu = jnp.where(q == 0, new_uv, vu_b2[at])
        new_vv = jnp.where(q == lane - 1, vu_back[at], vv_back[at])
        new_vv = jnp.where(q == lane, vv_b1up[at], new_vv)
        new_vv = jnp.where(first, vv[at], new_vv)
        new_vv = jnp.where(second & (q == at), uv_b1up[at] if at else uu_back[at], new_vv)
        out.append((new_uu, new_uv, new_vu, new_vv))
    return tuple(zip(*out))


def solve(uu, uv, vu, vv):
    tall = (2 * BLK, BLK)
    row, lane = iota(tall, 0), iota(tall, 1)
    q_u = jnp.where(row == lane, 1.0, 0.0).astype(F32)
    q_v = jnp.where(row == 2 * BLK - 1 - lane, 1.0, 0.0).astype(F32)
    for round_index in range(ROUNDS):
        cos, sin = angles(round_index, uu, uv, vv)
        q_u, q_v = q_u * cos - q_v * sin, q_u * sin + q_v * cos
        if round_index + 1 == ROUNDS:
            break
        near = [jnp.broadcast_to(x, (ROWS, BLK)) for x in (cos, sin)]
        new = []
        for at in range(2):
            far_cos, far_sin = (pltpu.roll(x, at, 1, stride=2, stride_axis=0) for x in near)
            a, b, c, d = uu[at], uv[at], vu[at], vv[at]
            a, b = a * far_cos - b * far_sin, a * far_sin + b * far_cos
            c, d = c * far_cos - d * far_sin, c * far_sin + d * far_cos
            a, c = a * cos - c * sin, a * sin + c * cos
            b, d = b * cos - d * sin, b * sin + d * cos
            new.append((a, b, c, d))
        uu, uv, vu, vv = shift_pairs(*zip(*new))
        q_u, q_v = (
            jnp.where(lane == BLK - 1, q_v, next_lane(q_u)),
            jnp.where(lane == 0, q_v, jnp.where(lane == 1, previous_lane(q_u), previous_lane(q_v))),
        )
    return q_u, q_v


def block_columns(q_u, q_v, lower):
    last_round = ROUNDS - 1
    lane = iota((1, BLK), 1)
    upper_index = jnp.where(lane >= last_round, lane - last_round, last_round - lane)
    from_u = jnp.where(lane < last_round, BLK - last_round + lane, 0)
    from_v = jnp.where(lane == BLK - 1, 0, BLK - 1 + last_round - lane)
    lower_index = jnp.where(lane < last_round, from_u, from_v)
    index = jnp.where(lower, lower_index, upper_index)
    first = lane < last_round
    in_u = (first & lower) | (jnp.logical_not(first) & jnp.logical_not(lower))
    return jnp.where(in_u, lanes(q_u, index), lanes(q_v, index))


def kernel(
    rows, pairs,
    s_in, f_in, s_out, f_out,
    s_own, f_own, s_half, f_half, s_pair, f_pair, s_split, f_split, s_done, f_done, bands, place, total,
    load_sem, store_sem, sum_send, sum_recv, move_send, move_recv,
):
    row, col = lax.axis_index("row"), lax.axis_index("col")
    last = pairs - 1

    load_s = pltpu.make_async_copy(s_in, s_own, load_sem.at[0])
    load_f = pltpu.make_async_copy(f_in, f_own, load_sem.at[1])
    load_s.start()
    load_f.start()

    up_to = jnp.where(col == 0, 1, jnp.where(col == last, last - 1, jnp.where(col == last - 1, last, col + 2)))
    up_pair = jnp.where(col >= last - 1, 1, 0)
    up_half = jnp.where(col == last, 1, 0)
    low_to = jnp.where(col == 0, 2, jnp.where(col == 1, 0, col - 2))
    low_pair = jnp.where(col <= 1, 0, 1)
    low_half = jnp.where(col == 0, 0, 1)
    stays_a = jnp.where(col == 0, 0, 1)
    stays_b = jnp.where(col == 0, 1, 0)
    half_b = jnp.where(col == last, 1, 0)

    barrier = pltpu.get_barrier_semaphore()
    peers = [lax.rem(row + rows // 2 * (d % 2) + d // 2, rows) for d in range(rows - 1, 0, -1)]
    with jax.named_scope("greet"):
        for peer in peers:
            pl.semaphore_signal(barrier, inc=1, device_id={"row": peer}, device_id_type=MESH)
        for partner in (up_to, low_to):
            pl.semaphore_signal(barrier, inc=1, device_id={"col": partner}, device_id_type=MESH)

    def send(at, source, target, peer):
        return pltpu.make_async_remote_copy(
            src_ref=source, dst_ref=target, send_sem=sum_send.at[at], recv_sem=sum_recv.at[at],
            device_id={"row": peer}, device_id_type=MESH,
        )

    def share(at):
        own = bands.at[at, row]
        for peer in peers:
            send(at, own, own, peer).start()

    def form(at, upper, lower):
        for block, packed in enumerate(gram_bands(upper, lower, place)):
            bands[at, row, KEPT * block:KEPT * (block + 1)] = packed

    def summed(at):
        rest = bands.at[at, pl.ds(0, rows - 1)]
        with jax.named_scope("sum_wait"):
            send(at, rest, rest, peers[0]).wait_recv()
        whole = bands[at, 0]
        for d in range(1, rows):
            whole = whole + bands[at, d]
        total[at, 0:4 * KEPT] = whole
        return [unpack(total[at, KEPT * block:KEPT * block + ROWS]) for block in range(4)]

    total[...] = jnp.zeros(total.shape, F32)
    with jax.named_scope("load_slab"):
        load_s.wait()
    with jax.named_scope("gram_first"):
        form(0, s_own[:, :BLK], s_own[:, BLK:])
    with jax.named_scope("entry"):
        pl.semaphore_wait(barrier, rows + 1)
    share(0)
    blocks = summed(0)
    with jax.named_scope("solve_first"):
        q_u, q_v = solve(*blocks)
        split = [halves(block_columns(q_u, q_v, lower)) for lower in (False, True)]
        split = [jnp.concatenate(parts, axis=1) for parts in zip(*split)]

    def move(kind, half, at, target, pair, half_at, to):
        return pltpu.make_async_remote_copy(
            src_ref=half.at[at], dst_ref=target.at[pair, half_at],
            send_sem=move_send.at[kind, at], recv_sem=move_recv.at[kind, pair],
            device_id={"col": to}, device_id_type=MESH,
        )

    def moves(kind, half, target):
        return (
            move(kind, half, 0, target, up_pair, up_half, up_to),
            move(kind, half, 1, target, low_pair, low_half, low_to),
        )

    def rotate(own, half, target):
        moved = times(halves(own[...]), split)
        half[0] = moved[:, :BLK]
        half[1] = moved[:, BLK:]

    def stay(half, target):
        target[0, stays_a] = half[stays_a]
        target[1, half_b] = half[stays_b]

    s_moves, f_moves = moves(0, s_half, s_pair), moves(1, f_half, f_pair)
    with jax.named_scope("apply_slab"):
        rotate(s_own, s_half, s_pair)
    for copy in s_moves:
        copy.start()
    load_f.wait()
    with jax.named_scope("apply_factor"):
        stay(s_half, s_pair)
        rotate(f_own, f_half, f_pair)
        stay(f_half, f_pair)

    def arrived(kind, half, target, pair):
        move(kind, half, 0, target, pair, 0, up_to).wait_recv()

    for pair in range(2):
        with jax.named_scope("slab_arrival"):
            arrived(0, s_half, s_pair, pair)
        with jax.named_scope("gram_second"):
            form(1 + pair, s_pair[pair, 0], s_pair[pair, 1])
        share(1 + pair)
    for copy in f_moves:
        copy.start()

    lower_of = (col == 1, col != last)

    def keep_halves(target, pair, split):
        whole = jnp.concatenate([target[pair, 0], target[pair, 1]], axis=1)
        split[0, pair], split[1, pair] = halves(whole)

    def finish(split, done, pair, rotation):
        done[:, pair * BLK:(pair + 1) * BLK] = times((split[0, pair], split[1, pair]), rotation)

    with jax.named_scope("split_slab"):
        for pair in range(2):
            keep_halves(s_pair, pair, s_split)
    for pair in range(2):
        blocks = summed(1 + pair)
        with jax.named_scope("solve_second"):
            q_u, q_v = solve(*blocks)
            rotation = halves(block_columns(q_u, q_v, lower_of[pair]))
        with jax.named_scope("finish_slab"):
            finish(s_split, s_done, pair, rotation)
        if pair == 0:
            for at in range(2):
                with jax.named_scope("factor_arrival"):
                    arrived(1, f_half, f_pair, at)
                with jax.named_scope("split_factor"):
                    keep_halves(f_pair, at, f_split)
        with jax.named_scope("finish_factor"):
            finish(f_split, f_done, pair, rotation)
    store_s = pltpu.make_async_copy(s_done, s_out, store_sem.at[0])
    store_f = pltpu.make_async_copy(f_done, f_out, store_sem.at[1])
    store_s.start()
    store_f.start()

    with jax.named_scope("last_waits"):
        for copy in s_moves + f_moves:
            copy.wait_send()
        for at in range(3):
            rest = bands.at[at, pl.ds(0, rows - 1)]
            send(at, rest, rest, peers[0]).wait_send()
        store_s.wait()
        store_f.wait()


def store(s_done, f_done, s_out, f_out, sem):
    copies = [
        pltpu.make_async_copy(source, target, sem.at[at])
        for at, (source, target) in enumerate(((s_done, s_out), (f_done, f_out)))
    ]
    for copy in copies:
        copy.start()
    for copy in copies:
        copy.wait()


def solution(mesh):
    rows, pairs = mesh.shape["row"], mesh.shape["col"]

    def shards(matrix, right_factor):
        s_rows, f_rows = matrix.shape[0], right_factor.shape[0]
        done = pl.pallas_call(
            lambda *refs: kernel(rows, pairs, *refs),
            out_shape=(
                pltpu.VMEM(matrix.shape, F32),
                pltpu.VMEM(right_factor.shape, F32),
            ),
            in_specs=[pl.BlockSpec(memory_space=pl.ANY)] * 2,
            out_specs=[pl.BlockSpec(memory_space=pl.ANY)] * 2,
            scratch_shapes=[
                pltpu.VMEM(matrix.shape, F32),
                pltpu.VMEM(right_factor.shape, F32),
                pltpu.VMEM((2, s_rows, BLK), F32),
                pltpu.VMEM((2, f_rows, BLK), F32),
                pltpu.VMEM((2, 2, s_rows, BLK), F32),
                pltpu.VMEM((2, 2, f_rows, BLK), F32),
                pltpu.VMEM((2, 2, s_rows, 2 * BLK), jnp.bfloat16),
                pltpu.VMEM((2, 2, f_rows, 2 * BLK), jnp.bfloat16),
                pltpu.VMEM(matrix.shape, F32),
                pltpu.VMEM(right_factor.shape, F32),
                pltpu.VMEM((3, rows, 4 * KEPT, BLK), F32),
                pltpu.VMEM((4, 2 * ROWS, BLK), F32),
                pltpu.VMEM((3, 4 * ROWS, BLK), F32),
                pltpu.SemaphoreType.DMA((2,)),
                pltpu.SemaphoreType.DMA((2,)),
                pltpu.SemaphoreType.DMA((3,)),
                pltpu.SemaphoreType.DMA((3,)),
                pltpu.SemaphoreType.DMA((2, 2)),
                pltpu.SemaphoreType.DMA((2, 2)),
            ],
            compiler_params=pltpu.CompilerParams(collective_id=0, has_side_effects=True, vmem_limit_bytes=GRANT),
            name="tournament",
        )(*[pltpu.with_memory_space_constraint(x, pltpu.HBM) for x in (matrix, right_factor)])
        return pl.pallas_call(
            store,
            out_shape=(pltpu.HBM(matrix.shape, F32), pltpu.HBM(right_factor.shape, F32)),
            in_specs=[pl.BlockSpec(memory_space=pl.ANY)] * 2,
            out_specs=[pl.BlockSpec(memory_space=pl.ANY)] * 2,
            scratch_shapes=[pltpu.SemaphoreType.DMA((2,))],
            compiler_params=pltpu.CompilerParams(vmem_limit_bytes=GRANT),
            name="store",
        )(*[pltpu.with_memory_space_constraint(x, pltpu.VMEM) for x in done])

    spec = P("row", "col")
    return jax.shard_map(shards, mesh=mesh, in_specs=(spec, spec), out_specs=(spec, spec), check_vma=False)
```

```python
import jax
import jax.numpy as jnp
from jax import lax
from jax.experimental import pallas as pl
from jax.experimental.pallas import tpu as pltpu
from jax.sharding import PartitionSpec as P

BLK = 128
ROUNDS = 6
ROWS = 8
TALL = 16
KEPT = 6
GRANT = 32 * 1024 * 1024
MESH = pl.DeviceIdType.MESH
F32 = jnp.float32


def iota(shape, axis):
    return lax.broadcasted_iota(jnp.int32, shape, axis)


def next_lane(x):
    return pltpu.roll(x, BLK - 1, 1)


def previous_lane(x):
    return pltpu.roll(x, 1, 1)


def below(x, n):
    even, odd = x
    up_even, up_odd = pltpu.roll(even, ROWS - 1, 0), pltpu.roll(odd, ROWS - 1, 0)
    return (odd, up_even) if n == 1 else (up_even, up_odd)


def above(x, n):
    even, odd = x
    down_even, down_odd = pltpu.roll(even, 1, 0), pltpu.roll(odd, 1, 0)
    return (down_odd, even) if n == 1 else (down_even, down_odd)


def both(function, *operands):
    return tuple(function(*parts) for parts in zip(*operands))


def lanes(x, index):
    return jnp.take_along_axis(x, jnp.broadcast_to(index, x.shape), axis=1)


def halves(x):
    high = x.astype(jnp.bfloat16)
    return high, (x - high.astype(F32)).astype(jnp.bfloat16)


def dot(x, y):
    return jnp.dot(x, y, preferred_element_type=F32)


def thirds(x):
    high, rest = halves(x)
    return high, rest, (x - high.astype(F32) - rest.astype(F32)).astype(jnp.bfloat16)


def times(x_split, split):
    x_high, x_low = x_split
    high, low = split[:2]
    width = high.shape[1]
    if width == BLK:
        beside = jnp.concatenate([high, low], axis=1)
        first, second = dot(x_high, beside), dot(x_low, beside)
        small = first[:, width:] + (second[:, :width] + second[:, width:])
        large = first[:, :width]
    else:
        small = dot(x_low, high) + dot(x_high, low)
        large = dot(x_high, high)
    if len(split) == 3:
        small = small + dot(x_high, split[2])
    return large + small


def products(x, y):
    x_parts, y_parts = thirds(x.T), thirds(y)
    count = x.shape[1]
    by_high = dot(jnp.concatenate(x_parts, axis=0), y_parts[0])
    by_middle = dot(jnp.concatenate(x_parts[:2], axis=0), y_parts[1])
    smallest = by_high[2 * count:] + by_middle[count:] + dot(x_parts[0], y_parts[2])
    return by_high[:count] + ((by_high[count:2 * count] + by_middle[:count]) + smallest)


def backwards(x):
    return lanes(x, BLK - 1 - iota((1, BLK), 1))


def diagonals(x, place):
    place[...] = pltpu.roll(x, 1, 1, stride=1, stride_axis=0).T[:2 * ROWS]
    return place[pl.ds(0, ROWS, stride=2)], place[pl.ds(1, ROWS, stride=2)]


def flipped_rows(x):
    index = jnp.clip(KEPT - 1 - iota(x.shape, 0), 0, ROWS - 1)
    return jnp.take_along_axis(x, index, axis=0)


def pack(even, odd):
    j, lane = iota((ROWS, BLK), 0), iota((ROWS, BLK), 1)
    odd = flipped_rows(odd)
    high = pltpu.roll(odd, 0, 1, stride=1, stride_axis=0)
    low = pltpu.roll(pltpu.roll(odd, 0, 1, stride=3, stride_axis=0), BLK - 11, 1)
    return jnp.where(lane < j, high, jnp.where(lane < 2 * j, low, even))[:KEPT]


def unpack(packed):
    i, lane = iota((ROWS, BLK), 0), iota((ROWS, BLK), 1)
    back = flipped_rows(packed)
    high = pltpu.roll(pltpu.roll(back, 0, 1, stride=1, stride_axis=0), BLK - 5, 1)
    low = pltpu.roll(pltpu.roll(back, 0, 1, stride=3, stride_axis=0), BLK - 4, 1)
    return packed, jnp.where(lane >= BLK - 5 + i, high, low)


def gram_bands(upper, lower, place):
    left = jnp.concatenate([upper, backwards(lower)], axis=1)
    right = jnp.concatenate([backwards(upper), lower], axis=1)
    gram = products(left, right)
    blocks = (gram[:BLK, :BLK], gram[:BLK, BLK:], gram[BLK:, :BLK], gram[BLK:, BLK:])
    return [pack(*diagonals(block, place.at[at])) for at, block in enumerate(blocks)]


def angles(round_index, uu, uv, vv):
    lane = iota((1, BLK), 1)
    spread = vv[0][0:1] - uu[0][0:1]
    across = 2.0 * uv[0][0:1]
    width = jnp.abs(spread)
    scale = jnp.maximum(jnp.abs(across), width)
    live = scale > 0
    inverse = 1.0 / jnp.where(live, scale, 1.0)
    across = across * inverse
    width = jnp.where(live, width * inverse, 1.0)
    root = lax.rsqrt(across * across + width * width)
    square = 0.5 + 0.5 * width * root
    root_cosine = lax.rsqrt(square)
    cosine = square * root_cosine
    sine = 0.5 * across * root * root_cosine
    upper_first = (lane == 0) | (lane > round_index)
    positive = (spread > 0) | ((spread == 0) & upper_first)
    return cosine, jnp.where(positive, sine, -sine)


def shift_pairs(uu, uv, vu, vv):
    lane, row = iota((ROWS, BLK), 1), iota((ROWS, BLK), 0)
    last, first, second = lane == BLK - 1, lane == 0, lane == 1
    uu_next, uv_next = both(next_lane, uu), both(next_lane, uv)
    uu_back, uv_back, vu_back, vv_back = (both(previous_lane, x) for x in (uu, uv, vu, vv))
    vu_1, vv_b1, uv_n1 = above(vu, 1), below(vv, 1), below(uv_next, 1)
    uu_n2, uv_n2, vu_b2, vv_b1up = below(uu_next, 2), below(uv_next, 2), above(vu_back, 2), above(vv_back, 1)
    uv_b1up = above(uv_back, 1)
    out = []
    for at in range(2):
        q = 2 * row + at
        new_uu = jnp.where(last, vu_1[at] if at else jnp.where(q == 0, vv[at], vu_1[at]), uu_next[at])
        new_uv = jnp.where(q == lane - 1, uu_n2[at], uv_n2[at])
        new_uv = jnp.where(q == lane, uv_n1[at], new_uv)
        new_uv = jnp.where(last, vv_b1[at], new_uv)
        if at:
            new_vu = jnp.where(q == 1, jnp.where(second, uu[at], uv[at]), vu_b2[at])
        else:
            new_vu = jnp.where(q == 0, new_uv, vu_b2[at])
        new_vv = jnp.where(q == lane - 1, vu_back[at], vv_back[at])
        new_vv = jnp.where(q == lane, vv_b1up[at], new_vv)
        new_vv = jnp.where(first, vv[at], new_vv)
        new_vv = jnp.where(second & (q == at), uv_b1up[at] if at else uu_back[at], new_vv)
        out.append((new_uu, new_uv, new_vu, new_vv))
    return tuple(zip(*out))


def turn_columns(part, cos, sin):
    to_u, to_v = part
    return to_u * cos - to_v * sin, to_u * sin + to_v * cos


def shift_columns(part):
    to_u, to_v = part
    lane = iota((TALL, BLK), 1)
    moved_u = pltpu.roll(next_lane(to_u), 1, 0)
    moved_v = pltpu.roll(jnp.where(lane == 1, previous_lane(to_u), previous_lane(to_v)), TALL - 1, 0)
    return jnp.where(lane == BLK - 1, to_v, moved_u), jnp.where(lane == 0, to_v, moved_v)


def solve(uu, uv, vu, vv):
    one = jnp.where(iota((TALL, BLK), 0) == ROWS, 1.0, 0.0).astype(F32)
    none = jnp.zeros((TALL, BLK), F32)
    parts = [(one, none), (none, one)]
    for round_index in range(ROUNDS):
        cos, sin = angles(round_index, uu, uv, vv)
        parts = [turn_columns(part, cos, sin) for part in parts]
        if round_index + 1 == ROUNDS:
            break
        near = [jnp.broadcast_to(x, (ROWS, BLK)) for x in (cos, sin)]
        new = []
        for at in range(2):
            far_cos, far_sin = (pltpu.roll(x, at, 1, stride=2, stride_axis=0) for x in near)
            a, b, c, d = uu[at], uv[at], vu[at], vv[at]
            a, b = a * far_cos - b * far_sin, a * far_sin + b * far_cos
            c, d = c * far_cos - d * far_sin, c * far_sin + d * far_cos
            a, c = a * cos - c * sin, a * sin + c * cos
            b, d = b * cos - d * sin, b * sin + d * cos
            new.append((a, b, c, d))
        uu, uv, vu, vv = shift_pairs(*zip(*new))
        parts = [shift_columns(part) for part in parts]
    return parts


def column_places(lower):
    last_round = ROUNDS - 1
    lane = iota((1, BLK), 1)
    upper_place = jnp.where(lane >= last_round, lane - last_round, last_round - lane)
    from_u = BLK - last_round + lane
    from_v = jnp.where(lane == BLK - 1, 0, BLK - 1 + last_round - lane)
    place = jnp.where(lower, jnp.where(lane < last_round, from_u, from_v), upper_place)
    first = lane < last_round
    in_u = (first & lower) | (jnp.logical_not(first) & jnp.logical_not(lower))
    return in_u, place


def block_columns(parts, lower):
    in_u, place = column_places(lower)
    return [jnp.where(in_u, lanes(to_u, place), lanes(to_v, place)) for to_u, to_v in parts]


def spread_rows(near, start):
    tall = jnp.concatenate([near, jnp.zeros((ROWS, BLK), F32)], axis=0)
    for bit in (1, 2, 4):
        tall = jnp.where((start & bit) != 0, pltpu.roll(tall, bit, 0), tall)
    tile = start >> 3
    out = []
    for at in range(BLK // ROWS):
        rows = jnp.where(tile == at - 1, tall[2 * ROWS:], 0.0)
        rows = jnp.where(tile == at, tall[ROWS:2 * ROWS], rows)
        out.append(jnp.where(tile == at + 1, tall[:ROWS], rows))
    return out


def whole_columns(near, lower):
    place = column_places(lower)[1]
    from_u, from_v = near
    flip = ROWS - 1 - iota((ROWS, BLK), 0)
    from_v = [jnp.take_along_axis(x, flip, axis=0) for x in (from_v[ROWS:], from_v[:ROWS])]
    tiles = spread_rows(from_u, place) + spread_rows(jnp.concatenate(from_v, axis=0), BLK - place)
    return jnp.concatenate(tiles, axis=0)


def kernel(
    rows, pairs,
    s_in, f_in, s_out, f_out,
    s_own, f_own, s_half, f_half, s_pair, f_pair, s_split, f_split, s_done, f_done, bands, place, total,
    s_other, columns_own, columns_in,
    load_sem, store_sem, sum_send, sum_recv, move_send, move_recv,
):
    load_s = pltpu.make_async_copy(s_in, s_own, load_sem.at[0])
    load_f = pltpu.make_async_copy(f_in, f_own, load_sem.at[1])
    with jax.named_scope("loads"):
        load_s.start()
        load_f.start()
    row, col = lax.axis_index("row"), lax.axis_index("col")
    last = pairs - 1

    up_to = jnp.where(col == 0, 1, jnp.where(col == last, last - 1, jnp.where(col == last - 1, last, col + 2)))
    up_pair = jnp.where(col >= last - 1, 1, 0)
    up_half = jnp.where(col == last, 1, 0)
    low_to = jnp.where(col == 0, 2, jnp.where(col == 1, 0, col - 2))
    low_pair = jnp.where(col <= 1, 0, 1)
    low_half = jnp.where(col == 0, 0, 1)
    stays_a = jnp.where(col == 0, 0, 1)
    stays_b = jnp.where(col == 0, 1, 0)
    own_half = (stays_a, jnp.where(col == last, 1, 0))
    other_lower = ((col == 0) | (col == 2), col < last - 1)

    barrier = pltpu.get_barrier_semaphore()
    peers = [lax.rem(row + rows // 2 * (d % 2) + d // 2, rows) for d in range(rows - 1, 0, -1)]
    with jax.named_scope("greet"):
        for peer in peers:
            pl.semaphore_signal(barrier, inc=1, device_id={"row": peer}, device_id_type=MESH)
        for partner in (up_to, low_to):
            pl.semaphore_signal(barrier, inc=1, device_id={"col": partner}, device_id_type=MESH)

    def send(at, source, target, peer):
        return pltpu.make_async_remote_copy(
            src_ref=source, dst_ref=target, send_sem=sum_send.at[at], recv_sem=sum_recv.at[at],
            device_id={"row": peer}, device_id_type=MESH,
        )

    def share(at):
        own = bands.at[at, row]
        for peer in peers:
            send(at, own, own, peer).start()

    def form(at, upper, lower):
        for block, packed in enumerate(gram_bands(upper, lower, place)):
            bands[at, row, KEPT * block:KEPT * (block + 1)] = packed

    def summed(at):
        rest = bands.at[at, pl.ds(0, rows - 1)]
        with jax.named_scope("sum_wait"):
            send(at, rest, rest, peers[0]).wait_recv()
        whole = bands[at, 0]
        for d in range(1, rows):
            whole = whole + bands[at, d]
        total[at, 0:4 * KEPT] = whole
        return [unpack(total[at, KEPT * block:KEPT * block + ROWS]) for block in range(4)]

    total[...] = jnp.zeros(total.shape, F32)
    with jax.named_scope("load_slab"):
        load_s.wait()
    with jax.named_scope("gram_first"):
        form(0, s_own[:, :BLK], s_own[:, BLK:])
    with jax.named_scope("entry"):
        pl.semaphore_wait(barrier, rows + 1)
    share(0)

    def move(kind, at, source, target, pair, to):
        return pltpu.make_async_remote_copy(
            src_ref=source, dst_ref=target, send_sem=move_send.at[kind, at], recv_sem=move_recv.at[kind, pair],
            device_id={"col": to}, device_id_type=MESH,
        )

    s_moves = [
        move(0, at, s_own, s_other.at[pair], pair, to)
        for at, (pair, to) in enumerate(((up_pair, up_to), (low_pair, low_to)))
    ]
    for copy in s_moves:
        copy.start()
    blocks = summed(0)
    with jax.named_scope("solve_first"):
        parts = solve(*blocks)
        columns = [block_columns(parts, lower) for lower in (False, True)]
        for at, near in enumerate(columns):
            columns_own[at, :TALL], columns_own[at, TALL:] = near
    column_moves = [
        move(2, at, columns_own.at[at], columns_in.at[pair], pair, to)
        for at, (pair, to) in enumerate(((up_pair, up_to), (low_pair, low_to)))
    ]
    for copy in column_moves:
        copy.start()
    with jax.named_scope("rotation_first"):
        split = thirds(
            jnp.concatenate([whole_columns(near, lower) for near, lower in zip(columns, (False, True))], axis=1)
        )

    def rotate(own, half, parts):
        moved = times(halves(own[...]), parts)
        half[0] = moved[:, :BLK]
        half[1] = moved[:, BLK:]

    def stay(half, target):
        target[0, own_half[0]] = half[stays_a]
        target[1, own_half[1]] = half[stays_b]

    f_moves = [
        move(1, 0, f_half.at[0], f_pair.at[up_pair, up_half], up_pair, up_to),
        move(1, 1, f_half.at[1], f_pair.at[low_pair, low_half], low_pair, low_to),
    ]
    with jax.named_scope("apply_slab"):
        rotate(s_own, s_half, split)
        stay(s_half, s_pair)
    load_f.wait()
    with jax.named_scope("apply_factor"):
        rotate(f_own, f_half, split[:2])
        stay(f_half, f_pair)

    def arrived(kind, target, pair):
        move(kind, 0, target, target, pair, up_to).wait_recv()

    def keep_halves(whole, pair, split):
        split[0, pair], split[1, pair] = halves(whole)

    for pair in range(2):
        with jax.named_scope("slab_arrival"):
            arrived(0, s_other.at[pair], pair)
        with jax.named_scope("split_other"):
            keep_halves(s_other[pair], pair, s_split)
    def pick(choices, at):
        return jnp.where(at == 0, choices[0], choices[1])

    first = jnp.where((col == pairs // 2) | (col == pairs // 2 + 1), 1, 0)
    order = (first, 1 - first)
    for pair in order:
        with jax.named_scope("columns_arrival"):
            arrived(2, columns_in.at[pair], pair)
        with jax.named_scope("rotation_other"):
            near = [columns_in[pair, :TALL], columns_in[pair, TALL:]]
            rotation = thirds(whole_columns(near, pick(other_lower, pair)))
        with jax.named_scope("apply_other"):
            s_pair[pair, 1 - pick(own_half, pair)] = times((s_split[0, pair], s_split[1, pair]), rotation)
        with jax.named_scope("gram_second"):
            form(1 + pair, s_pair[pair, 0], s_pair[pair, 1])
        share(1 + pair)
    for copy in f_moves:
        copy.start()

    lower_of = (col == 1, col != last)

    def joined(target, pair):
        return jnp.concatenate([target[pair, 0], target[pair, 1]], axis=1)

    def finish(split, done, pair, rotation):
        at = pl.ds(pl.multiple_of(pair * BLK, BLK), BLK)
        done[:, at] = times((split[0, pair], split[1, pair]), rotation)

    with jax.named_scope("split_slab"):
        for pair in range(2):
            keep_halves(joined(s_pair, pair), pair, s_split)
    for step, pair in enumerate(order):
        blocks = summed(1 + pair)
        with jax.named_scope("solve_second"):
            parts = solve(*blocks)
        with jax.named_scope("rotation_second"):
            lower = pick(lower_of, pair)
            rotation = halves(whole_columns(block_columns(parts, lower), lower))
        with jax.named_scope("finish_slab"):
            finish(s_split, s_done, pair, rotation)
        if step == 0:
            for at in range(2):
                with jax.named_scope("factor_arrival"):
                    arrived(1, f_half.at[0], at)
                with jax.named_scope("split_factor"):
                    keep_halves(joined(f_pair, at), at, f_split)
        with jax.named_scope("finish_factor"):
            finish(f_split, f_done, pair, rotation)
    store_s = pltpu.make_async_copy(s_done, s_out, store_sem.at[0])
    store_f = pltpu.make_async_copy(f_done, f_out, store_sem.at[1])
    store_s.start()
    store_f.start()

    with jax.named_scope("last_waits"):
        for copy in s_moves + column_moves + f_moves:
            copy.wait_send()
        for at in range(3):
            rest = bands.at[at, pl.ds(0, rows - 1)]
            send(at, rest, rest, peers[0]).wait_send()
        store_s.wait()
        store_f.wait()


def store(s_done, f_done, s_out, f_out, sem):
    copies = [
        pltpu.make_async_copy(source, target, sem.at[at])
        for at, (source, target) in enumerate(((s_done, s_out), (f_done, f_out)))
    ]
    for copy in copies:
        copy.start()
    for copy in copies:
        copy.wait()


def solution(mesh):
    rows, pairs = mesh.shape["row"], mesh.shape["col"]

    def shards(matrix, right_factor):
        s_rows, f_rows = matrix.shape[0], right_factor.shape[0]
        done = pl.pallas_call(
            lambda *refs: kernel(rows, pairs, *refs),
            out_shape=(
                pltpu.VMEM(matrix.shape, F32),
                pltpu.VMEM(right_factor.shape, F32),
            ),
            in_specs=[pl.BlockSpec(memory_space=pl.ANY)] * 2,
            out_specs=[pl.BlockSpec(memory_space=pl.ANY)] * 2,
            scratch_shapes=[
                pltpu.VMEM(matrix.shape, F32),
                pltpu.VMEM(right_factor.shape, F32),
                pltpu.VMEM((2, s_rows, BLK), F32),
                pltpu.VMEM((2, f_rows, BLK), F32),
                pltpu.VMEM((2, 2, s_rows, BLK), F32),
                pltpu.VMEM((2, 2, f_rows, BLK), F32),
                pltpu.VMEM((2, 2, s_rows, 2 * BLK), jnp.bfloat16),
                pltpu.VMEM((2, 2, f_rows, 2 * BLK), jnp.bfloat16),
                pltpu.VMEM(matrix.shape, F32),
                pltpu.VMEM(right_factor.shape, F32),
                pltpu.VMEM((3, rows, 4 * KEPT, BLK), F32),
                pltpu.VMEM((4, 2 * ROWS, BLK), F32),
                pltpu.VMEM((3, 4 * ROWS, BLK), F32),
                pltpu.VMEM((2,) + matrix.shape, F32),
                pltpu.VMEM((2, 2 * TALL, BLK), F32),
                pltpu.VMEM((2, 2 * TALL, BLK), F32),
                pltpu.SemaphoreType.DMA((2,)),
                pltpu.SemaphoreType.DMA((2,)),
                pltpu.SemaphoreType.DMA((3,)),
                pltpu.SemaphoreType.DMA((3,)),
                pltpu.SemaphoreType.DMA((3, 2)),
                pltpu.SemaphoreType.DMA((3, 2)),
            ],
            compiler_params=pltpu.CompilerParams(collective_id=0, has_side_effects=True, vmem_limit_bytes=GRANT),
            name="tournament",
        )(*[pltpu.with_memory_space_constraint(x, pltpu.HBM) for x in (matrix, right_factor)])
        return pl.pallas_call(
            store,
            out_shape=(pltpu.HBM(matrix.shape, F32), pltpu.HBM(right_factor.shape, F32)),
            in_specs=[pl.BlockSpec(memory_space=pl.ANY)] * 2,
            out_specs=[pl.BlockSpec(memory_space=pl.ANY)] * 2,
            scratch_shapes=[pltpu.SemaphoreType.DMA((2,))],
            compiler_params=pltpu.CompilerParams(vmem_limit_bytes=GRANT),
            name="store",
        )(*[pltpu.with_memory_space_constraint(x, pltpu.VMEM) for x in done])

    spec = P("row", "col")
    return jax.shard_map(shards, mesh=mesh, in_specs=(spec, spec), out_specs=(spec, spec), check_vma=False)
```

```python
import jax
import jax.numpy as jnp
from jax import lax
from jax.experimental import pallas as pl
from jax.experimental.pallas import tpu as pltpu
from jax.sharding import PartitionSpec as P

BLK = 128
ROUNDS = 6
ROWS = 8
TALL = 16
KEPT = 6
GRANT = 32 * 1024 * 1024
MESH = pl.DeviceIdType.MESH
F32 = jnp.float32


def iota(shape, axis):
    return lax.broadcasted_iota(jnp.int32, shape, axis)


def next_lane(x):
    return pltpu.roll(x, BLK - 1, 1)


def previous_lane(x):
    return pltpu.roll(x, 1, 1)


def below(x, n):
    even, odd = x
    up_even, up_odd = pltpu.roll(even, ROWS - 1, 0), pltpu.roll(odd, ROWS - 1, 0)
    return (odd, up_even) if n == 1 else (up_even, up_odd)


def above(x, n):
    even, odd = x
    down_even, down_odd = pltpu.roll(even, 1, 0), pltpu.roll(odd, 1, 0)
    return (down_odd, even) if n == 1 else (down_even, down_odd)


def both(function, *operands):
    return tuple(function(*parts) for parts in zip(*operands))


def lanes(x, index):
    return jnp.take_along_axis(x, jnp.broadcast_to(index, x.shape), axis=1)


def halves(x):
    high = x.astype(jnp.bfloat16)
    return high, (x - high.astype(F32)).astype(jnp.bfloat16)


def dot(x, y):
    return jnp.dot(x, y, preferred_element_type=F32)


def thirds(x):
    high, rest = halves(x)
    return high, rest, (x - high.astype(F32) - rest.astype(F32)).astype(jnp.bfloat16)


def times(x_split, split):
    x_high, x_low = x_split
    high, low = split[:2]
    width = high.shape[1]
    if width == BLK:
        beside = jnp.concatenate([high, low], axis=1)
        first, second = dot(x_high, beside), dot(x_low, beside)
        small = first[:, width:] + (second[:, :width] + second[:, width:])
        large = first[:, :width]
    else:
        small = dot(x_low, high) + dot(x_high, low)
        large = dot(x_high, high)
    if len(split) == 3:
        small = small + dot(x_high, split[2])
    return large + small


def products(x, y):
    x_parts, y_parts = thirds(x.T), thirds(y)
    count = x.shape[1]
    by_high = dot(jnp.concatenate(x_parts, axis=0), y_parts[0])
    by_middle = dot(jnp.concatenate(x_parts[:2], axis=0), y_parts[1])
    smallest = by_high[2 * count:] + by_middle[count:] + dot(x_parts[0], y_parts[2])
    return by_high[:count] + ((by_high[count:2 * count] + by_middle[:count]) + smallest)


def backwards(x):
    return lanes(x, BLK - 1 - iota((1, BLK), 1))


def diagonals(blocks, place):
    lane = iota((BLK, BLK), 1)
    beside = pltpu.roll(blocks[0], 1, 1, stride=1, stride_axis=0)
    for at, block in enumerate(blocks[1:], 1):
        turned = pltpu.roll(block, 1 + at * TALL, 1, stride=1, stride_axis=0)
        beside = jnp.where(lane >= at * TALL, turned, beside)
    place[...] = beside.T[:len(blocks) * TALL]
    return [
        tuple(place[pl.ds(at * TALL + odd, ROWS, stride=2)] for odd in range(2)) for at in range(len(blocks))
    ]


def flipped_rows(x):
    index = jnp.clip(KEPT - 1 - iota(x.shape, 0), 0, ROWS - 1)
    return jnp.take_along_axis(x, index, axis=0)


def pack(even, odd):
    j, lane = iota((ROWS, BLK), 0), iota((ROWS, BLK), 1)
    odd = flipped_rows(odd)
    high = pltpu.roll(odd, 0, 1, stride=1, stride_axis=0)
    low = pltpu.roll(pltpu.roll(odd, 0, 1, stride=3, stride_axis=0), BLK - 11, 1)
    return jnp.where(lane < j, high, jnp.where(lane < 2 * j, low, even))[:KEPT]


def unpack(packed):
    i, lane = iota((ROWS, BLK), 0), iota((ROWS, BLK), 1)
    back = flipped_rows(packed)
    high = pltpu.roll(pltpu.roll(back, 0, 1, stride=1, stride_axis=0), BLK - 5, 1)
    low = pltpu.roll(pltpu.roll(back, 0, 1, stride=3, stride_axis=0), BLK - 4, 1)
    return packed, jnp.where(lane >= BLK - 5 + i, high, low)


def gram_bands(upper, lower, place):
    left = jnp.concatenate([upper, backwards(lower)], axis=1)
    right = jnp.concatenate([backwards(upper), lower], axis=1)
    gram = products(left, right)
    blocks = (gram[:BLK, :BLK], gram[:BLK, BLK:], gram[BLK:, :BLK], gram[BLK:, BLK:])
    return [pack(*pair) for pair in diagonals(blocks, place)]


def angles(round_index, uu, uv, vv):
    lane = iota((1, BLK), 1)
    spread = vv[0][0:1] - uu[0][0:1]
    across = 2.0 * uv[0][0:1]
    width = jnp.abs(spread)
    scale = jnp.maximum(jnp.abs(across), width)
    live = scale > 0
    inverse = 1.0 / jnp.where(live, scale, 1.0)
    across = across * inverse
    width = jnp.where(live, width * inverse, 1.0)
    root = lax.rsqrt(across * across + width * width)
    square = 0.5 + 0.5 * width * root
    root_cosine = lax.rsqrt(square)
    cosine = square * root_cosine
    sine = 0.5 * across * root * root_cosine
    upper_first = (lane == 0) | (lane > round_index)
    positive = (spread > 0) | ((spread == 0) & upper_first)
    return cosine, jnp.where(positive, sine, -sine)


def shift_pairs(uu, uv, vu, vv):
    lane, row = iota((ROWS, BLK), 1), iota((ROWS, BLK), 0)
    last, first, second = lane == BLK - 1, lane == 0, lane == 1
    uu_next, uv_next = both(next_lane, uu), both(next_lane, uv)
    uu_back, uv_back, vu_back, vv_back = (both(previous_lane, x) for x in (uu, uv, vu, vv))
    vu_1, vv_b1, uv_n1 = above(vu, 1), below(vv, 1), below(uv_next, 1)
    uu_n2, uv_n2, vu_b2, vv_b1up = below(uu_next, 2), below(uv_next, 2), above(vu_back, 2), above(vv_back, 1)
    uv_b1up = above(uv_back, 1)
    out = []
    for at in range(2):
        q = 2 * row + at
        new_uu = jnp.where(last, vu_1[at] if at else jnp.where(q == 0, vv[at], vu_1[at]), uu_next[at])
        new_uv = jnp.where(q == lane - 1, uu_n2[at], uv_n2[at])
        new_uv = jnp.where(q == lane, uv_n1[at], new_uv)
        new_uv = jnp.where(last, vv_b1[at], new_uv)
        if at:
            new_vu = jnp.where(q == 1, jnp.where(second, uu[at], uv[at]), vu_b2[at])
        else:
            new_vu = jnp.where(q == 0, new_uv, vu_b2[at])
        new_vv = jnp.where(q == lane - 1, vu_back[at], vv_back[at])
        new_vv = jnp.where(q == lane, vv_b1up[at], new_vv)
        new_vv = jnp.where(first, vv[at], new_vv)
        new_vv = jnp.where(second & (q == at), uv_b1up[at] if at else uu_back[at], new_vv)
        out.append((new_uu, new_uv, new_vu, new_vv))
    return tuple(zip(*out))


def turn_columns(part, cos, sin):
    to_u, to_v = part
    return to_u * cos - to_v * sin, to_u * sin + to_v * cos


def shift_columns(part):
    to_u, to_v = part
    lane = iota((TALL, BLK), 1)
    moved_u = pltpu.roll(next_lane(to_u), 1, 0)
    moved_v = pltpu.roll(jnp.where(lane == 1, previous_lane(to_u), previous_lane(to_v)), TALL - 1, 0)
    return jnp.where(lane == BLK - 1, to_v, moved_u), jnp.where(lane == 0, to_v, moved_v)


def solve(uu, uv, vu, vv):
    one = jnp.where(iota((TALL, BLK), 0) == ROWS, 1.0, 0.0).astype(F32)
    none = jnp.zeros((TALL, BLK), F32)
    parts = ((one, none), (none, one))

    def turn(round_index, state):
        (uu, uv, vu, vv), parts = state
        cos, sin = angles(round_index, uu, uv, vv)
        parts = tuple(turn_columns(part, cos, sin) for part in parts)
        near = [jnp.broadcast_to(x, (ROWS, BLK)) for x in (cos, sin)]
        new = []
        for at in range(2):
            far_cos, far_sin = (pltpu.roll(x, at, 1, stride=2, stride_axis=0) for x in near)
            a, b, c, d = uu[at], uv[at], vu[at], vv[at]
            a, b = a * far_cos - b * far_sin, a * far_sin + b * far_cos
            c, d = c * far_cos - d * far_sin, c * far_sin + d * far_cos
            a, c = a * cos - c * sin, a * sin + c * cos
            b, d = b * cos - d * sin, b * sin + d * cos
            new.append((a, b, c, d))
        return shift_pairs(*zip(*new)), tuple(shift_columns(part) for part in parts)

    blocks, parts = lax.fori_loop(0, ROUNDS - 1, turn, ((uu, uv, vu, vv), parts))
    cos, sin = angles(ROUNDS - 1, blocks[0], blocks[1], blocks[3])
    return [turn_columns(part, cos, sin) for part in parts]


def column_places(lower):
    last_round = ROUNDS - 1
    lane = iota((1, BLK), 1)
    upper_place = jnp.where(lane >= last_round, lane - last_round, last_round - lane)
    from_u = BLK - last_round + lane
    from_v = jnp.where(lane == BLK - 1, 0, BLK - 1 + last_round - lane)
    place = jnp.where(lower, jnp.where(lane < last_round, from_u, from_v), upper_place)
    first = lane < last_round
    in_u = (first & lower) | (jnp.logical_not(first) & jnp.logical_not(lower))
    return in_u, place


def block_columns(parts, lower):
    in_u, place = column_places(lower)
    return [jnp.where(in_u, lanes(to_u, place), lanes(to_v, place)) for to_u, to_v in parts]


def spread_rows(near, start):
    tall = jnp.concatenate([near, jnp.zeros((ROWS, BLK), F32)], axis=0)
    for bit in (1, 2, 4):
        tall = jnp.where((start & bit) != 0, pltpu.roll(tall, bit, 0), tall)
    tile = start >> 3
    out = []
    for at in range(BLK // ROWS):
        rows = jnp.where(tile == at - 1, tall[2 * ROWS:], 0.0)
        rows = jnp.where(tile == at, tall[ROWS:2 * ROWS], rows)
        out.append(jnp.where(tile == at + 1, tall[:ROWS], rows))
    return out


def whole_columns(near, lower):
    place = column_places(lower)[1]
    from_u, from_v = near
    flip = ROWS - 1 - iota((ROWS, BLK), 0)
    from_v = [jnp.take_along_axis(x, flip, axis=0) for x in (from_v[ROWS:], from_v[:ROWS])]
    tiles = spread_rows(from_u, place) + spread_rows(jnp.concatenate(from_v, axis=0), BLK - place)
    return jnp.concatenate(tiles, axis=0)


def kernel(
    rows, pairs,
    s_in, f_in, s_out, f_out,
    s_own, f_own, s_half, f_half, s_pair, f_pair, s_split, f_split, s_done, f_done, bands, place, total,
    s_other, columns_own, columns_in,
    load_sem, store_sem, sum_send, sum_recv, move_send, move_recv,
):
    load_s = pltpu.make_async_copy(s_in, s_own, load_sem.at[0])
    load_f = pltpu.make_async_copy(f_in, f_own, load_sem.at[1])
    with jax.named_scope("loads"):
        load_s.start()
        load_f.start()
    row, col = lax.axis_index("row"), lax.axis_index("col")
    last = pairs - 1

    up_to = jnp.where(col == 0, 1, jnp.where(col == last, last - 1, jnp.where(col == last - 1, last, col + 2)))
    up_pair = jnp.where(col >= last - 1, 1, 0)
    up_half = jnp.where(col == last, 1, 0)
    low_to = jnp.where(col == 0, 2, jnp.where(col == 1, 0, col - 2))
    low_pair = jnp.where(col <= 1, 0, 1)
    low_half = jnp.where(col == 0, 0, 1)
    stays_a = jnp.where(col == 0, 0, 1)
    stays_b = jnp.where(col == 0, 1, 0)
    own_half = (stays_a, jnp.where(col == last, 1, 0))
    other_lower = ((col == 0) | (col == 2), col < last - 1)

    barrier = pltpu.get_barrier_semaphore()
    ring = rows // 2
    side, place_at = row // ring, lax.rem(row, ring)
    steps = [(across, step) for step in range(ring) for across in (1, 0) if across or step]
    steps.sort(key=lambda s: -min(s[1], ring - s[1]))
    peers = [lax.rem(side + across, 2) * ring + lax.rem(place_at + step, ring) for across, step in steps]
    with jax.named_scope("greet"):
        for peer in peers:
            pl.semaphore_signal(barrier, inc=1, device_id={"row": peer}, device_id_type=MESH)
        for partner in (up_to, low_to):
            pl.semaphore_signal(barrier, inc=1, device_id={"col": partner}, device_id_type=MESH)

    def send(at, source, target, peer):
        return pltpu.make_async_remote_copy(
            src_ref=source, dst_ref=target, send_sem=sum_send.at[at], recv_sem=sum_recv.at[at],
            device_id={"row": peer}, device_id_type=MESH,
        )

    def share(at):
        own = bands.at[at, row]
        for peer in peers:
            send(at, own, own, peer).start()

    def form(at, upper, lower):
        for block, packed in enumerate(gram_bands(upper, lower, place)):
            bands[at, row, KEPT * block:KEPT * (block + 1)] = packed

    def summed(at):
        rest = bands.at[at, pl.ds(0, rows - 1)]
        with jax.named_scope("sum_wait"):
            send(at, rest, rest, peers[0]).wait_recv()
        whole = bands[at, 0]
        for d in range(1, rows):
            whole = whole + bands[at, d]
        total[at, 0:4 * KEPT] = whole
        return [unpack(total[at, KEPT * block:KEPT * block + ROWS]) for block in range(4)]

    total[...] = jnp.zeros(total.shape, F32)
    with jax.named_scope("load_slab"):
        load_s.wait()
    with jax.named_scope("gram_first"):
        form(0, s_own[:, :BLK], s_own[:, BLK:])
    with jax.named_scope("entry"):
        pl.semaphore_wait(barrier, rows + 1)
    share(0)

    def move(kind, at, source, target, pair, to):
        return pltpu.make_async_remote_copy(
            src_ref=source, dst_ref=target, send_sem=move_send.at[kind, at], recv_sem=move_recv.at[kind, pair],
            device_id={"col": to}, device_id_type=MESH,
        )

    s_moves = [
        move(0, at, s_own, s_other.at[pair], pair, to)
        for at, (pair, to) in enumerate(((up_pair, up_to), (low_pair, low_to)))
    ]
    for copy in s_moves:
        copy.start()
    blocks = summed(0)
    with jax.named_scope("solve_first"):
        parts = solve(*blocks)
        columns = [block_columns(parts, lower) for lower in (False, True)]
        for at, near in enumerate(columns):
            columns_own[at, :TALL], columns_own[at, TALL:] = near
    column_moves = [
        move(2, at, columns_own.at[at], columns_in.at[pair], pair, to)
        for at, (pair, to) in enumerate(((up_pair, up_to), (low_pair, low_to)))
    ]
    for copy in column_moves:
        copy.start()
    with jax.named_scope("rotation_first"):
        split = thirds(
            jnp.concatenate([whole_columns(near, lower) for near, lower in zip(columns, (False, True))], axis=1)
        )

    def rotate(own, half, parts):
        moved = times(halves(own[...]), parts)
        half[0] = moved[:, :BLK]
        half[1] = moved[:, BLK:]

    def stay(half, target):
        target[0, own_half[0]] = half[stays_a]
        target[1, own_half[1]] = half[stays_b]

    f_moves = [
        move(1, 0, f_half.at[0], f_pair.at[up_pair, up_half], up_pair, up_to),
        move(1, 1, f_half.at[1], f_pair.at[low_pair, low_half], low_pair, low_to),
    ]
    with jax.named_scope("apply_slab"):
        rotate(s_own, s_half, split)
        stay(s_half, s_pair)
    load_f.wait()
    with jax.named_scope("apply_factor"):
        rotate(f_own, f_half, split[:2])
        stay(f_half, f_pair)

    def arrived(kind, target, pair):
        move(kind, 0, target, target, pair, up_to).wait_recv()

    def keep_halves(whole, pair, split):
        split[0, pair], split[1, pair] = halves(whole)

    for pair in range(2):
        with jax.named_scope("slab_arrival"):
            arrived(0, s_other.at[pair], pair)
        with jax.named_scope("split_other"):
            keep_halves(s_other[pair], pair, s_split)
    def pick(choices, at):
        return jnp.where(at == 0, choices[0], choices[1])

    first = jnp.where((col >= pairs // 2) & (col < pairs // 2 + 4), 1, 0)
    order = (first, 1 - first)
    for pair in order:
        with jax.named_scope("columns_arrival"):
            arrived(2, columns_in.at[pair], pair)
        with jax.named_scope("rotation_other"):
            near = [columns_in[pair, :TALL], columns_in[pair, TALL:]]
            rotation = thirds(whole_columns(near, pick(other_lower, pair)))
        with jax.named_scope("apply_other"):
            s_pair[pair, 1 - pick(own_half, pair)] = times((s_split[0, pair], s_split[1, pair]), rotation)
        with jax.named_scope("gram_second"):
            form(1 + pair, s_pair[pair, 0], s_pair[pair, 1])
        share(1 + pair)
    for copy in f_moves:
        copy.start()

    lower_of = (col == 1, col != last)

    def joined(target, pair):
        return jnp.concatenate([target[pair, 0], target[pair, 1]], axis=1)

    def finish(split, done, pair, rotation):
        at = pl.ds(pl.multiple_of(pair * BLK, BLK), BLK)
        done[:, at] = times((split[0, pair], split[1, pair]), rotation)

    with jax.named_scope("split_slab"):
        for pair in range(2):
            keep_halves(joined(s_pair, pair), pair, s_split)
    for pair in order:
        blocks = summed(1 + pair)
        with jax.named_scope("solve_second"):
            parts = solve(*blocks)
        with jax.named_scope("rotation_second"):
            lower = pick(lower_of, pair)
            rotation = halves(whole_columns(block_columns(parts, lower), lower))
        with jax.named_scope("finish_slab"):
            finish(s_split, s_done, pair, rotation)
        with jax.named_scope("factor_arrival"):
            arrived(1, f_half.at[0], pair)
        with jax.named_scope("split_factor"):
            keep_halves(joined(f_pair, pair), pair, f_split)
        with jax.named_scope("finish_factor"):
            finish(f_split, f_done, pair, rotation)
    store_s = pltpu.make_async_copy(s_done, s_out, store_sem.at[0])
    store_f = pltpu.make_async_copy(f_done, f_out, store_sem.at[1])
    store_s.start()
    store_f.start()

    with jax.named_scope("last_waits"):
        for copy in s_moves + column_moves + f_moves:
            copy.wait_send()
        for at in range(3):
            rest = bands.at[at, pl.ds(0, rows - 1)]
            send(at, rest, rest, peers[0]).wait_send()
        store_s.wait()
        store_f.wait()


def store(s_done, f_done, s_out, f_out, sem):
    copies = [
        pltpu.make_async_copy(source, target, sem.at[at])
        for at, (source, target) in enumerate(((s_done, s_out), (f_done, f_out)))
    ]
    for copy in copies:
        copy.start()
    for copy in copies:
        copy.wait()


def solution(mesh):
    rows, pairs = mesh.shape["row"], mesh.shape["col"]

    def shards(matrix, right_factor):
        s_rows, f_rows = matrix.shape[0], right_factor.shape[0]
        done = pl.pallas_call(
            lambda *refs: kernel(rows, pairs, *refs),
            out_shape=(
                pltpu.VMEM(matrix.shape, F32),
                pltpu.VMEM(right_factor.shape, F32),
            ),
            in_specs=[pl.BlockSpec(memory_space=pl.ANY)] * 2,
            out_specs=[pl.BlockSpec(memory_space=pl.ANY)] * 2,
            scratch_shapes=[
                pltpu.VMEM(matrix.shape, F32),
                pltpu.VMEM(right_factor.shape, F32),
                pltpu.VMEM((2, s_rows, BLK), F32),
                pltpu.VMEM((2, f_rows, BLK), F32),
                pltpu.VMEM((2, 2, s_rows, BLK), F32),
                pltpu.VMEM((2, 2, f_rows, BLK), F32),
                pltpu.VMEM((2, 2, s_rows, 2 * BLK), jnp.bfloat16),
                pltpu.VMEM((2, 2, f_rows, 2 * BLK), jnp.bfloat16),
                pltpu.VMEM(matrix.shape, F32),
                pltpu.VMEM(right_factor.shape, F32),
                pltpu.VMEM((3, rows, 4 * KEPT, BLK), F32),
                pltpu.VMEM((4 * TALL, BLK), F32),
                pltpu.VMEM((3, 4 * ROWS, BLK), F32),
                pltpu.VMEM((2,) + matrix.shape, F32),
                pltpu.VMEM((2, 2 * TALL, BLK), F32),
                pltpu.VMEM((2, 2 * TALL, BLK), F32),
                pltpu.SemaphoreType.DMA((2,)),
                pltpu.SemaphoreType.DMA((2,)),
                pltpu.SemaphoreType.DMA((3,)),
                pltpu.SemaphoreType.DMA((3,)),
                pltpu.SemaphoreType.DMA((3, 2)),
                pltpu.SemaphoreType.DMA((3, 2)),
            ],
            compiler_params=pltpu.CompilerParams(collective_id=0, has_side_effects=True, vmem_limit_bytes=GRANT),
            name="tournament",
        )(*[pltpu.with_memory_space_constraint(x, pltpu.HBM) for x in (matrix, right_factor)])
        return pl.pallas_call(
            store,
            out_shape=(pltpu.HBM(matrix.shape, F32), pltpu.HBM(right_factor.shape, F32)),
            in_specs=[pl.BlockSpec(memory_space=pl.ANY)] * 2,
            out_specs=[pl.BlockSpec(memory_space=pl.ANY)] * 2,
            scratch_shapes=[pltpu.SemaphoreType.DMA((2,))],
            compiler_params=pltpu.CompilerParams(vmem_limit_bytes=GRANT),
            name="store",
        )(*[pltpu.with_memory_space_constraint(x, pltpu.VMEM) for x in done])

    spec = P("row", "col")
    return jax.shard_map(shards, mesh=mesh, in_specs=(spec, spec), out_specs=(spec, spec), check_vma=False)
```

```python
import jax
import jax.numpy as jnp
from jax import lax
from jax.experimental import pallas as pl
from jax.experimental.pallas import tpu as pltpu
from jax.sharding import PartitionSpec as P

BLK = 128
ROUNDS = 6
ROWS = 8
TALL = 16
KEPT = 6
GRANT = 32 * 1024 * 1024
MESH = pl.DeviceIdType.MESH
F32 = jnp.float32


def iota(shape, axis):
    return lax.broadcasted_iota(jnp.int32, shape, axis)


def next_lane(x):
    return pltpu.roll(x, BLK - 1, 1)


def previous_lane(x):
    return pltpu.roll(x, 1, 1)


def below(x, n):
    even, odd = x
    up_even, up_odd = pltpu.roll(even, ROWS - 1, 0), pltpu.roll(odd, ROWS - 1, 0)
    return (odd, up_even) if n == 1 else (up_even, up_odd)


def above(x, n):
    even, odd = x
    down_even, down_odd = pltpu.roll(even, 1, 0), pltpu.roll(odd, 1, 0)
    return (down_odd, even) if n == 1 else (down_even, down_odd)


def both(function, *operands):
    return tuple(function(*parts) for parts in zip(*operands))


def lanes(x, index):
    return jnp.take_along_axis(x, jnp.broadcast_to(index, x.shape), axis=1)


def halves(x):
    high = x.astype(jnp.bfloat16)
    return high, (x - high.astype(F32)).astype(jnp.bfloat16)


def dot(x, y):
    return jnp.dot(x, y, preferred_element_type=F32)


def thirds(x):
    high, rest = halves(x)
    return high, rest, (x - high.astype(F32) - rest.astype(F32)).astype(jnp.bfloat16)


def times(x_split, split):
    x_high, x_low = x_split
    high, low = split[:2]
    width = high.shape[1]
    if width == BLK:
        beside = jnp.concatenate([high, low], axis=1)
        first, second = dot(x_high, beside), dot(x_low, beside)
        small = first[:, width:] + (second[:, :width] + second[:, width:])
        large = first[:, :width]
    else:
        small = dot(x_low, high) + dot(x_high, low)
        large = dot(x_high, high)
    if len(split) == 3:
        small = small + dot(x_high, split[2])
    return large + small


def products(x, y):
    x_parts, y_parts = thirds(x.T), thirds(y)
    count = x.shape[1]
    by_high = dot(jnp.concatenate(x_parts, axis=0), y_parts[0])
    by_middle = dot(jnp.concatenate(x_parts[:2], axis=0), y_parts[1])
    smallest = by_high[2 * count:] + by_middle[count:] + dot(x_parts[0], y_parts[2])
    return by_high[:count] + ((by_high[count:2 * count] + by_middle[:count]) + smallest)


def backwards(x):
    return lanes(x, BLK - 1 - iota((1, BLK), 1))


def diagonals(blocks, place):
    lane = iota((BLK, BLK), 1)
    beside = pltpu.roll(blocks[0], 1, 1, stride=1, stride_axis=0)
    for at, block in enumerate(blocks[1:], 1):
        turned = pltpu.roll(block, 1 + at * TALL, 1, stride=1, stride_axis=0)
        beside = jnp.where(lane >= at * TALL, turned, beside)
    place[...] = beside.T[:len(blocks) * TALL]
    return [
        tuple(place[pl.ds(at * TALL + odd, ROWS, stride=2)] for odd in range(2)) for at in range(len(blocks))
    ]


def flipped_rows(x):
    index = jnp.clip(KEPT - 1 - iota(x.shape, 0), 0, ROWS - 1)
    return jnp.take_along_axis(x, index, axis=0)


def pack(even, odd):
    j, lane = iota((ROWS, BLK), 0), iota((ROWS, BLK), 1)
    odd = flipped_rows(odd)
    high = pltpu.roll(odd, 0, 1, stride=1, stride_axis=0)
    low = pltpu.roll(pltpu.roll(odd, 0, 1, stride=3, stride_axis=0), BLK - 11, 1)
    return jnp.where(lane < j, high, jnp.where(lane < 2 * j, low, even))[:KEPT]


def unpack(packed):
    i, lane = iota((ROWS, BLK), 0), iota((ROWS, BLK), 1)
    back = flipped_rows(packed)
    high = pltpu.roll(pltpu.roll(back, 0, 1, stride=1, stride_axis=0), BLK - 5, 1)
    low = pltpu.roll(pltpu.roll(back, 0, 1, stride=3, stride_axis=0), BLK - 4, 1)
    return packed, jnp.where(lane >= BLK - 5 + i, high, low)


def gram_bands(upper, lower, place):
    left = jnp.concatenate([upper, backwards(lower)], axis=1)
    right = jnp.concatenate([backwards(upper), lower], axis=1)
    gram = products(left, right)
    blocks = (gram[:BLK, :BLK], gram[:BLK, BLK:], gram[BLK:, :BLK], gram[BLK:, BLK:])
    return [pack(*pair) for pair in diagonals(blocks, place)]


def angles(round_index, uu, uv, vv):
    lane = iota((1, BLK), 1)
    spread = vv[0][0:1] - uu[0][0:1]
    across = 2.0 * uv[0][0:1]
    width = jnp.abs(spread)
    scale = jnp.maximum(jnp.abs(across), width)
    live = scale > 0
    inverse = 1.0 / jnp.where(live, scale, 1.0)
    across = across * inverse
    width = jnp.where(live, width * inverse, 1.0)
    root = lax.rsqrt(across * across + width * width)
    square = 0.5 + 0.5 * width * root
    root_cosine = lax.rsqrt(square)
    cosine = square * root_cosine
    sine = 0.5 * across * root * root_cosine
    upper_first = (lane == 0) | (lane > round_index)
    positive = (spread > 0) | ((spread == 0) & upper_first)
    return cosine, jnp.where(positive, sine, -sine)


def shift_pairs(uu, uv, vu, vv):
    lane, row = iota((ROWS, BLK), 1), iota((ROWS, BLK), 0)
    last, first, second = lane == BLK - 1, lane == 0, lane == 1
    uu_next, uv_next = both(next_lane, uu), both(next_lane, uv)
    uu_back, uv_back, vu_back, vv_back = (both(previous_lane, x) for x in (uu, uv, vu, vv))
    vu_1, vv_b1, uv_n1 = above(vu, 1), below(vv, 1), below(uv_next, 1)
    uu_n2, uv_n2, vu_b2, vv_b1up = below(uu_next, 2), below(uv_next, 2), above(vu_back, 2), above(vv_back, 1)
    uv_b1up = above(uv_back, 1)
    out = []
    for at in range(2):
        q = 2 * row + at
        new_uu = jnp.where(last, vu_1[at] if at else jnp.where(q == 0, vv[at], vu_1[at]), uu_next[at])
        new_uv = jnp.where(q == lane - 1, uu_n2[at], uv_n2[at])
        new_uv = jnp.where(q == lane, uv_n1[at], new_uv)
        new_uv = jnp.where(last, vv_b1[at], new_uv)
        if at:
            new_vu = jnp.where(q == 1, jnp.where(second, uu[at], uv[at]), vu_b2[at])
        else:
            new_vu = jnp.where(q == 0, new_uv, vu_b2[at])
        new_vv = jnp.where(q == lane - 1, vu_back[at], vv_back[at])
        new_vv = jnp.where(q == lane, vv_b1up[at], new_vv)
        new_vv = jnp.where(first, vv[at], new_vv)
        new_vv = jnp.where(second & (q == at), uv_b1up[at] if at else uu_back[at], new_vv)
        out.append((new_uu, new_uv, new_vu, new_vv))
    return tuple(zip(*out))


def turn_columns(part, cos, sin):
    to_u, to_v = part
    return to_u * cos - to_v * sin, to_u * sin + to_v * cos


def shift_columns(part):
    to_u, to_v = part
    lane = iota((TALL, BLK), 1)
    moved_u = pltpu.roll(next_lane(to_u), 1, 0)
    moved_v = pltpu.roll(jnp.where(lane == 1, previous_lane(to_u), previous_lane(to_v)), TALL - 1, 0)
    return jnp.where(lane == BLK - 1, to_v, moved_u), jnp.where(lane == 0, to_v, moved_v)


def solve(uu, uv, vu, vv):
    one = jnp.where(iota((TALL, BLK), 0) == ROWS, 1.0, 0.0).astype(F32)
    none = jnp.zeros((TALL, BLK), F32)
    parts = ((one, none), (none, one))

    def turn(round_index, state):
        (uu, uv, vu, vv), parts = state
        cos, sin = angles(round_index, uu, uv, vv)
        parts = tuple(turn_columns(part, cos, sin) for part in parts)
        near = [jnp.broadcast_to(x, (ROWS, BLK)) for x in (cos, sin)]
        new = []
        for at in range(2):
            far_cos, far_sin = (pltpu.roll(x, at, 1, stride=2, stride_axis=0) for x in near)
            a, b, c, d = uu[at], uv[at], vu[at], vv[at]
            a, b = a * far_cos - b * far_sin, a * far_sin + b * far_cos
            c, d = c * far_cos - d * far_sin, c * far_sin + d * far_cos
            a, c = a * cos - c * sin, a * sin + c * cos
            b, d = b * cos - d * sin, b * sin + d * cos
            new.append((a, b, c, d))
        return shift_pairs(*zip(*new)), tuple(shift_columns(part) for part in parts)

    blocks, parts = lax.fori_loop(0, ROUNDS - 1, turn, ((uu, uv, vu, vv), parts))
    cos, sin = angles(ROUNDS - 1, blocks[0], blocks[1], blocks[3])
    return [turn_columns(part, cos, sin) for part in parts]


def column_places(lower):
    last_round = ROUNDS - 1
    lane = iota((1, BLK), 1)
    upper_place = jnp.where(lane >= last_round, lane - last_round, last_round - lane)
    from_u = BLK - last_round + lane
    from_v = jnp.where(lane == BLK - 1, 0, BLK - 1 + last_round - lane)
    place = jnp.where(lower, jnp.where(lane < last_round, from_u, from_v), upper_place)
    first = lane < last_round
    in_u = (first & lower) | (jnp.logical_not(first) & jnp.logical_not(lower))
    return in_u, place


def block_columns(parts, lower):
    in_u, place = column_places(lower)
    return [jnp.where(in_u, lanes(to_u, place), lanes(to_v, place)) for to_u, to_v in parts]


def spread_rows(near, start):
    tall = jnp.concatenate([near, jnp.zeros((ROWS, BLK), F32)], axis=0)
    for bit in (1, 2, 4):
        tall = jnp.where((start & bit) != 0, pltpu.roll(tall, bit, 0), tall)
    tile = start >> 3
    out = []
    for at in range(BLK // ROWS):
        rows = jnp.where(tile == at - 1, tall[2 * ROWS:], 0.0)
        rows = jnp.where(tile == at, tall[ROWS:2 * ROWS], rows)
        out.append(jnp.where(tile == at + 1, tall[:ROWS], rows))
    return out


def whole_columns(near, lower):
    place = column_places(lower)[1]
    from_u, from_v = near
    flip = ROWS - 1 - iota((ROWS, BLK), 0)
    from_v = [jnp.take_along_axis(x, flip, axis=0) for x in (from_v[ROWS:], from_v[:ROWS])]
    tiles = spread_rows(from_u, place) + spread_rows(jnp.concatenate(from_v, axis=0), BLK - place)
    return jnp.concatenate(tiles, axis=0)


def kernel(
    rows, pairs,
    s_in, f_in, s_out, f_out,
    s_own, f_own, s_half, f_half, s_pair, f_pair, s_split, f_split, s_done, f_done, bands, place, total,
    s_other, columns_own, columns_in,
    load_sem, store_sem, sum_send, sum_recv, move_send, move_recv,
):
    load_s = pltpu.make_async_copy(s_in, s_own, load_sem.at[0])
    load_f = pltpu.make_async_copy(f_in, f_own, load_sem.at[1])
    with jax.named_scope("loads"):
        load_s.start()
        load_f.start()
    row, col = lax.axis_index("row"), lax.axis_index("col")
    last = pairs - 1

    up_to = jnp.where(col == 0, 1, jnp.where(col == last, last - 1, jnp.where(col == last - 1, last, col + 2)))
    up_pair = jnp.where(col >= last - 1, 1, 0)
    up_half = jnp.where(col == last, 1, 0)
    low_to = jnp.where(col == 0, 2, jnp.where(col == 1, 0, col - 2))
    low_pair = jnp.where(col <= 1, 0, 1)
    low_half = jnp.where(col == 0, 0, 1)
    stays_a = jnp.where(col == 0, 0, 1)
    stays_b = jnp.where(col == 0, 1, 0)
    own_half = (stays_a, jnp.where(col == last, 1, 0))
    other_lower = ((col == 0) | (col == 2), col < last - 1)

    barrier = pltpu.get_barrier_semaphore()
    ring = rows // 2
    side, place_at = row // ring, lax.rem(row, ring)
    steps = [(across, step) for step in range(ring) for across in (1, 0) if across or step]
    steps.sort(key=lambda s: -min(s[1], ring - s[1]))
    peers = [lax.rem(side + across, 2) * ring + lax.rem(place_at + step, ring) for across, step in steps]
    with jax.named_scope("greet"):
        for peer in peers:
            pl.semaphore_signal(barrier, inc=1, device_id={"row": peer}, device_id_type=MESH)
        for partner in (up_to, low_to):
            pl.semaphore_signal(barrier, inc=1, device_id={"col": partner}, device_id_type=MESH)

    def send(at, source, target, peer):
        return pltpu.make_async_remote_copy(
            src_ref=source, dst_ref=target, send_sem=sum_send.at[at], recv_sem=sum_recv.at[at],
            device_id={"row": peer}, device_id_type=MESH,
        )

    def share(at):
        own = bands.at[at, row]
        for peer in peers:
            send(at, own, own, peer).start()

    def form(at, upper, lower):
        for block, packed in enumerate(gram_bands(upper, lower, place)):
            bands[at, row, KEPT * block:KEPT * (block + 1)] = packed

    def summed(at):
        rest = bands.at[at, pl.ds(0, rows - 1)]
        with jax.named_scope("sum_wait"):
            send(at, rest, rest, peers[0]).wait_recv()
        whole = bands[at, 0]
        for d in range(1, rows):
            whole = whole + bands[at, d]
        total[at, 0:4 * KEPT] = whole
        return [unpack(total[at, KEPT * block:KEPT * block + ROWS]) for block in range(4)]

    total[...] = jnp.zeros(total.shape, F32)
    with jax.named_scope("load_slab"):
        load_s.wait()
    with jax.named_scope("gram_first"):
        form(0, s_own[:, :BLK], s_own[:, BLK:])
    with jax.named_scope("entry"):
        pl.semaphore_wait(barrier, rows + 1)
    share(0)

    def move(kind, at, source, target, pair, to):
        return pltpu.make_async_remote_copy(
            src_ref=source, dst_ref=target, send_sem=move_send.at[kind, at], recv_sem=move_recv.at[kind, pair],
            device_id={"col": to}, device_id_type=MESH,
        )

    s_moves = [
        move(0, at, s_own, s_other.at[pair], pair, to)
        for at, (pair, to) in enumerate(((up_pair, up_to), (low_pair, low_to)))
    ]
    for copy in s_moves:
        copy.start()
    blocks = summed(0)
    with jax.named_scope("solve_first"):
        parts = solve(*blocks)
        columns = [block_columns(parts, lower) for lower in (False, True)]
        for at, near in enumerate(columns):
            columns_own[at, :TALL], columns_own[at, TALL:] = near
    column_moves = [
        move(2, at, columns_own.at[at], columns_in.at[pair], pair, to)
        for at, (pair, to) in enumerate(((up_pair, up_to), (low_pair, low_to)))
    ]
    for copy in column_moves:
        copy.start()
    with jax.named_scope("rotation_first"):
        split = thirds(
            jnp.concatenate([whole_columns(near, lower) for near, lower in zip(columns, (False, True))], axis=1)
        )

    def rotate(own, half, parts):
        moved = times(halves(own[...]), parts)
        half[0] = moved[:, :BLK]
        half[1] = moved[:, BLK:]

    def stay(half, target):
        target[0, own_half[0]] = half[stays_a]
        target[1, own_half[1]] = half[stays_b]

    f_moves = [
        move(1, 0, f_half.at[0], f_pair.at[up_pair, up_half], up_pair, up_to),
        move(1, 1, f_half.at[1], f_pair.at[low_pair, low_half], low_pair, low_to),
    ]
    with jax.named_scope("apply_slab"):
        rotate(s_own, s_half, split)
        stay(s_half, s_pair)
    load_f.wait()
    with jax.named_scope("apply_factor"):
        rotate(f_own, f_half, split[:2])
        stay(f_half, f_pair)

    def arrived(kind, target, pair):
        move(kind, 0, target, target, pair, up_to).wait_recv()

    def keep_halves(whole, pair, split):
        split[0, pair], split[1, pair] = halves(whole)

    def pick(choices, at):
        return jnp.where(at == 0, choices[0], choices[1])

    first = jnp.where((col >= pairs // 2) & (col < pairs // 2 + 4), 1, 0)
    order = (first, 1 - first)
    for pair in order:
        with jax.named_scope("slab_arrival"):
            arrived(0, s_other.at[pair], pair)
        with jax.named_scope("split_other"):
            keep_halves(s_other[pair], pair, s_split)
        with jax.named_scope("columns_arrival"):
            arrived(2, columns_in.at[pair], pair)
        with jax.named_scope("rotation_other"):
            near = [columns_in[pair, :TALL], columns_in[pair, TALL:]]
            rotation = thirds(whole_columns(near, pick(other_lower, pair)))
        with jax.named_scope("apply_other"):
            s_pair[pair, 1 - pick(own_half, pair)] = times((s_split[0, pair], s_split[1, pair]), rotation)
        with jax.named_scope("gram_second"):
            form(1 + pair, s_pair[pair, 0], s_pair[pair, 1])
        share(1 + pair)
    for copy in f_moves:
        copy.start()

    lower_of = (col == 1, col != last)

    def joined(target, pair):
        return jnp.concatenate([target[pair, 0], target[pair, 1]], axis=1)

    def finish(split, done, pair, rotation):
        at = pl.ds(pl.multiple_of(pair * BLK, BLK), BLK)
        done[:, at] = times((split[0, pair], split[1, pair]), rotation)

    with jax.named_scope("split_slab"):
        for pair in range(2):
            keep_halves(joined(s_pair, pair), pair, s_split)
    for pair in order:
        blocks = summed(1 + pair)
        with jax.named_scope("solve_second"):
            parts = solve(*blocks)
        with jax.named_scope("rotation_second"):
            lower = pick(lower_of, pair)
            rotation = halves(whole_columns(block_columns(parts, lower), lower))
        with jax.named_scope("finish_slab"):
            finish(s_split, s_done, pair, rotation)
        with jax.named_scope("factor_arrival"):
            arrived(1, f_half.at[0], pair)
        with jax.named_scope("split_factor"):
            keep_halves(joined(f_pair, pair), pair, f_split)
        with jax.named_scope("finish_factor"):
            finish(f_split, f_done, pair, rotation)
    store_s = pltpu.make_async_copy(s_done, s_out, store_sem.at[0])
    store_f = pltpu.make_async_copy(f_done, f_out, store_sem.at[1])
    store_s.start()
    store_f.start()

    with jax.named_scope("last_waits"):
        for copy in s_moves + column_moves + f_moves:
            copy.wait_send()
        for at in range(3):
            rest = bands.at[at, pl.ds(0, rows - 1)]
            send(at, rest, rest, peers[0]).wait_send()
        store_s.wait()
        store_f.wait()


def store(s_done, f_done, s_out, f_out, sem):
    copies = [
        pltpu.make_async_copy(source, target, sem.at[at])
        for at, (source, target) in enumerate(((s_done, s_out), (f_done, f_out)))
    ]
    for copy in copies:
        copy.start()
    for copy in copies:
        copy.wait()


def solution(mesh):
    rows, pairs = mesh.shape["row"], mesh.shape["col"]

    def shards(matrix, right_factor):
        s_rows, f_rows = matrix.shape[0], right_factor.shape[0]
        done = pl.pallas_call(
            lambda *refs: kernel(rows, pairs, *refs),
            out_shape=(
                pltpu.VMEM(matrix.shape, F32),
                pltpu.VMEM(right_factor.shape, F32),
            ),
            in_specs=[pl.BlockSpec(memory_space=pl.ANY)] * 2,
            out_specs=[pl.BlockSpec(memory_space=pl.ANY)] * 2,
            scratch_shapes=[
                pltpu.VMEM(matrix.shape, F32),
                pltpu.VMEM(right_factor.shape, F32),
                pltpu.VMEM((2, s_rows, BLK), F32),
                pltpu.VMEM((2, f_rows, BLK), F32),
                pltpu.VMEM((2, 2, s_rows, BLK), F32),
                pltpu.VMEM((2, 2, f_rows, BLK), F32),
                pltpu.VMEM((2, 2, s_rows, 2 * BLK), jnp.bfloat16),
                pltpu.VMEM((2, 2, f_rows, 2 * BLK), jnp.bfloat16),
                pltpu.VMEM(matrix.shape, F32),
                pltpu.VMEM(right_factor.shape, F32),
                pltpu.VMEM((3, rows, 4 * KEPT, BLK), F32),
                pltpu.VMEM((4 * TALL, BLK), F32),
                pltpu.VMEM((3, 4 * ROWS, BLK), F32),
                pltpu.VMEM((2,) + matrix.shape, F32),
                pltpu.VMEM((2, 2 * TALL, BLK), F32),
                pltpu.VMEM((2, 2 * TALL, BLK), F32),
                pltpu.SemaphoreType.DMA((2,)),
                pltpu.SemaphoreType.DMA((2,)),
                pltpu.SemaphoreType.DMA((3,)),
                pltpu.SemaphoreType.DMA((3,)),
                pltpu.SemaphoreType.DMA((3, 2)),
                pltpu.SemaphoreType.DMA((3, 2)),
            ],
            compiler_params=pltpu.CompilerParams(collective_id=0, has_side_effects=True, vmem_limit_bytes=GRANT),
            name="tournament",
        )(*[pltpu.with_memory_space_constraint(x, pltpu.HBM) for x in (matrix, right_factor)])
        return pl.pallas_call(
            store,
            out_shape=(pltpu.HBM(matrix.shape, F32), pltpu.HBM(right_factor.shape, F32)),
            in_specs=[pl.BlockSpec(memory_space=pl.ANY)] * 2,
            out_specs=[pl.BlockSpec(memory_space=pl.ANY)] * 2,
            scratch_shapes=[pltpu.SemaphoreType.DMA((2,))],
            compiler_params=pltpu.CompilerParams(vmem_limit_bytes=GRANT),
            name="store",
        )(*[pltpu.with_memory_space_constraint(x, pltpu.VMEM) for x in done])

    spec = P("row", "col")
    return jax.shard_map(shards, mesh=mesh, in_specs=(spec, spec), out_specs=(spec, spec), check_vma=False)
```

```python
import jax
import jax.numpy as jnp
from jax import lax
from jax.experimental import pallas as pl
from jax.experimental.pallas import tpu as pltpu
from jax.sharding import PartitionSpec as P

BLK = 128
ROUNDS = 6
ROWS = 8
TALL = 16
KEPT = 6
GRANT = 32 * 1024 * 1024
MESH = pl.DeviceIdType.MESH
F32 = jnp.float32


def iota(shape, axis):
    return lax.broadcasted_iota(jnp.int32, shape, axis)


def next_lane(x):
    return pltpu.roll(x, BLK - 1, 1)


def previous_lane(x):
    return pltpu.roll(x, 1, 1)


def below(x, n):
    even, odd = x
    up_even, up_odd = pltpu.roll(even, ROWS - 1, 0), pltpu.roll(odd, ROWS - 1, 0)
    return (odd, up_even) if n == 1 else (up_even, up_odd)


def above(x, n):
    even, odd = x
    down_even, down_odd = pltpu.roll(even, 1, 0), pltpu.roll(odd, 1, 0)
    return (down_odd, even) if n == 1 else (down_even, down_odd)


def both(function, *operands):
    return tuple(function(*parts) for parts in zip(*operands))


def lanes(x, index):
    return jnp.take_along_axis(x, jnp.broadcast_to(index, x.shape), axis=1)


def halves(x):
    high = x.astype(jnp.bfloat16)
    return high, (x - high.astype(F32)).astype(jnp.bfloat16)


def dot(x, y):
    return jnp.dot(x, y, preferred_element_type=F32)


def thirds(x):
    high, rest = halves(x)
    return high, rest, (x - high.astype(F32) - rest.astype(F32)).astype(jnp.bfloat16)


def times(x_split, split):
    x_high, x_low = x_split
    high, low = split[:2]
    width = high.shape[1]
    if width == BLK:
        beside = jnp.concatenate([high, low], axis=1)
        first, second = dot(x_high, beside), dot(x_low, beside)
        small = first[:, width:] + (second[:, :width] + second[:, width:])
        large = first[:, :width]
    else:
        small = dot(x_low, high) + dot(x_high, low)
        large = dot(x_high, high)
    if len(split) == 3:
        small = small + dot(x_high, split[2])
    return large + small


def products(x, y):
    x_parts, y_parts = thirds(x.T), thirds(y)
    count = x.shape[1]
    by_high = dot(jnp.concatenate(x_parts, axis=0), y_parts[0])
    by_middle = dot(jnp.concatenate(x_parts[:2], axis=0), y_parts[1])
    smallest = by_high[2 * count:] + by_middle[count:] + dot(x_parts[0], y_parts[2])
    return by_high[:count] + ((by_high[count:2 * count] + by_middle[:count]) + smallest)


def backwards(x):
    return lanes(x, BLK - 1 - iota((1, BLK), 1))


def diagonals(blocks, place):
    lane = iota((BLK, BLK), 1)
    beside = pltpu.roll(blocks[0], 1, 1, stride=1, stride_axis=0)
    for at, block in enumerate(blocks[1:], 1):
        turned = pltpu.roll(block, 1 + at * TALL, 1, stride=1, stride_axis=0)
        beside = jnp.where(lane >= at * TALL, turned, beside)
    place[:len(blocks) * TALL] = beside.T[:len(blocks) * TALL]
    return [
        tuple(place[pl.ds(at * TALL + odd, ROWS, stride=2)] for odd in range(2)) for at in range(len(blocks))
    ]


def flipped_rows(x):
    index = jnp.clip(KEPT - 1 - iota(x.shape, 0), 0, ROWS - 1)
    return jnp.take_along_axis(x, index, axis=0)


def pack(even, odd):
    j, lane = iota((ROWS, BLK), 0), iota((ROWS, BLK), 1)
    odd = flipped_rows(odd)
    high = pltpu.roll(odd, 0, 1, stride=1, stride_axis=0)
    low = pltpu.roll(pltpu.roll(odd, 0, 1, stride=3, stride_axis=0), BLK - 11, 1)
    return jnp.where(lane < j, high, jnp.where(lane < 2 * j, low, even))[:KEPT]


def unpack(packed):
    i, lane = iota((ROWS, BLK), 0), iota((ROWS, BLK), 1)
    back = flipped_rows(packed)
    high = pltpu.roll(pltpu.roll(back, 0, 1, stride=1, stride_axis=0), BLK - 5, 1)
    low = pltpu.roll(pltpu.roll(back, 0, 1, stride=3, stride_axis=0), BLK - 4, 1)
    return packed, jnp.where(lane >= BLK - 5 + i, high, low)


def gram_bands(upper, lower, place):
    left = jnp.concatenate([upper, backwards(lower)], axis=1)
    right = jnp.concatenate([backwards(upper), lower], axis=1)
    gram = products(left, right)
    blocks = (gram[:BLK, :BLK], gram[:BLK, BLK:], gram[BLK:, :BLK], gram[BLK:, BLK:])
    return [pack(*pair) for pair in diagonals(blocks, place)]


def angles(round_index, uu, uv, vv):
    lane = iota((1, BLK), 1)
    spread = vv[0][0:1] - uu[0][0:1]
    across = 2.0 * uv[0][0:1]
    width = jnp.abs(spread)
    scale = jnp.maximum(jnp.abs(across), width)
    live = scale > 0
    inverse = 1.0 / jnp.where(live, scale, 1.0)
    across = across * inverse
    width = jnp.where(live, width * inverse, 1.0)
    root = lax.rsqrt(across * across + width * width)
    square = 0.5 + 0.5 * width * root
    root_cosine = lax.rsqrt(square)
    cosine = square * root_cosine
    sine = 0.5 * across * root * root_cosine
    upper_first = (lane == 0) | (lane > round_index)
    positive = (spread > 0) | ((spread == 0) & upper_first)
    return cosine, jnp.where(positive, sine, -sine)


def shift_pairs(uu, uv, vu, vv):
    lane, row = iota((ROWS, BLK), 1), iota((ROWS, BLK), 0)
    last, first, second = lane == BLK - 1, lane == 0, lane == 1
    uu_next, uv_next = both(next_lane, uu), both(next_lane, uv)
    uu_back, uv_back, vu_back, vv_back = (both(previous_lane, x) for x in (uu, uv, vu, vv))
    vu_1, vv_b1, uv_n1 = above(vu, 1), below(vv, 1), below(uv_next, 1)
    uu_n2, uv_n2, vu_b2, vv_b1up = below(uu_next, 2), below(uv_next, 2), above(vu_back, 2), above(vv_back, 1)
    uv_b1up = above(uv_back, 1)
    out = []
    for at in range(2):
        q = 2 * row + at
        new_uu = jnp.where(last, vu_1[at] if at else jnp.where(q == 0, vv[at], vu_1[at]), uu_next[at])
        new_uv = jnp.where(q == lane - 1, uu_n2[at], uv_n2[at])
        new_uv = jnp.where(q == lane, uv_n1[at], new_uv)
        new_uv = jnp.where(last, vv_b1[at], new_uv)
        if at:
            new_vu = jnp.where(q == 1, jnp.where(second, uu[at], uv[at]), vu_b2[at])
        else:
            new_vu = jnp.where(q == 0, new_uv, vu_b2[at])
        new_vv = jnp.where(q == lane - 1, vu_back[at], vv_back[at])
        new_vv = jnp.where(q == lane, vv_b1up[at], new_vv)
        new_vv = jnp.where(first, vv[at], new_vv)
        new_vv = jnp.where(second & (q == at), uv_b1up[at] if at else uu_back[at], new_vv)
        out.append((new_uu, new_uv, new_vu, new_vv))
    return tuple(zip(*out))


def turn_columns(part, cos, sin):
    to_u, to_v = part
    return to_u * cos - to_v * sin, to_u * sin + to_v * cos


def shift_columns(part):
    to_u, to_v = part
    lane = iota((TALL, BLK), 1)
    moved_u = pltpu.roll(next_lane(to_u), 1, 0)
    moved_v = pltpu.roll(jnp.where(lane == 1, previous_lane(to_u), previous_lane(to_v)), TALL - 1, 0)
    return jnp.where(lane == BLK - 1, to_v, moved_u), jnp.where(lane == 0, to_v, moved_v)


def solve(uu, uv, vu, vv):
    one = jnp.where(iota((TALL, BLK), 0) == ROWS, 1.0, 0.0).astype(F32)
    none = jnp.zeros((TALL, BLK), F32)
    parts = ((one, none), (none, one))

    def turn(round_index, state):
        (uu, uv, vu, vv), parts = state
        cos, sin = angles(round_index, uu, uv, vv)
        parts = tuple(turn_columns(part, cos, sin) for part in parts)
        near = [jnp.broadcast_to(x, (ROWS, BLK)) for x in (cos, sin)]
        new = []
        for at in range(2):
            far_cos, far_sin = (pltpu.roll(x, at, 1, stride=2, stride_axis=0) for x in near)
            a, b, c, d = uu[at], uv[at], vu[at], vv[at]
            a, b = a * far_cos - b * far_sin, a * far_sin + b * far_cos
            c, d = c * far_cos - d * far_sin, c * far_sin + d * far_cos
            a, c = a * cos - c * sin, a * sin + c * cos
            b, d = b * cos - d * sin, b * sin + d * cos
            new.append((a, b, c, d))
        return shift_pairs(*zip(*new)), tuple(shift_columns(part) for part in parts)

    blocks, parts = lax.fori_loop(0, ROUNDS - 1, turn, ((uu, uv, vu, vv), parts))
    cos, sin = angles(ROUNDS - 1, blocks[0], blocks[1], blocks[3])
    return [turn_columns(part, cos, sin) for part in parts]


def column_places(lower):
    last_round = ROUNDS - 1
    lane = iota((1, BLK), 1)
    upper_place = jnp.where(lane >= last_round, lane - last_round, last_round - lane)
    from_u = BLK - last_round + lane
    from_v = jnp.where(lane == BLK - 1, 0, BLK - 1 + last_round - lane)
    place = jnp.where(lower, jnp.where(lane < last_round, from_u, from_v), upper_place)
    first = lane < last_round
    in_u = (first & lower) | (jnp.logical_not(first) & jnp.logical_not(lower))
    return in_u, place


def block_columns(parts, lower):
    in_u, place = column_places(lower)
    return [jnp.where(in_u, lanes(to_u, place), lanes(to_v, place)) for to_u, to_v in parts]


def spread_rows(near, start):
    tall = jnp.concatenate([near, jnp.zeros((ROWS, BLK), F32)], axis=0)
    for bit in (1, 2, 4):
        tall = jnp.where((start & bit) != 0, pltpu.roll(tall, bit, 0), tall)
    tile = start >> 3
    out = []
    for at in range(BLK // ROWS):
        rows = jnp.where(tile == at - 1, tall[2 * ROWS:], 0.0)
        rows = jnp.where(tile == at, tall[ROWS:2 * ROWS], rows)
        out.append(jnp.where(tile == at + 1, tall[:ROWS], rows))
    return out


def whole_columns(near, lower):
    place = column_places(lower)[1]
    from_u, from_v = near
    flip = ROWS - 1 - iota((ROWS, BLK), 0)
    from_v = [jnp.take_along_axis(x, flip, axis=0) for x in (from_v[ROWS:], from_v[:ROWS])]
    tiles = spread_rows(from_u, place) + spread_rows(jnp.concatenate(from_v, axis=0), BLK - place)
    return jnp.concatenate(tiles, axis=0)


def kernel(
    rows, pairs,
    s_in, f_in, s_out, f_out,
    s_own, f_own, s_half, f_half, s_pair, f_pair, s_split, f_split, s_done, f_done, bands, place, total,
    s_other, columns_own, columns_in,
    load_sem, store_sem, sum_send, sum_recv, move_send, move_recv,
):
    load_s = pltpu.make_async_copy(s_in, s_own, load_sem.at[0])
    load_f = pltpu.make_async_copy(f_in, f_own, load_sem.at[1])
    with jax.named_scope("loads"):
        load_s.start()
        load_f.start()
    row, col = lax.axis_index("row"), lax.axis_index("col")
    last = pairs - 1

    up_to = jnp.where(col == 0, 1, jnp.where(col == last, last - 1, jnp.where(col == last - 1, last, col + 2)))
    up_pair = jnp.where(col >= last - 1, 1, 0)
    up_half = jnp.where(col == last, 1, 0)
    low_to = jnp.where(col == 0, 2, jnp.where(col == 1, 0, col - 2))
    low_pair = jnp.where(col <= 1, 0, 1)
    low_half = jnp.where(col == 0, 0, 1)
    stays_a = jnp.where(col == 0, 0, 1)
    stays_b = jnp.where(col == 0, 1, 0)
    own_half = (stays_a, jnp.where(col == last, 1, 0))
    other_lower = ((col == 0) | (col == 2), col < last - 1)

    barrier = pltpu.get_barrier_semaphore()
    ring = rows // 2
    side, place_at = row // ring, lax.rem(row, ring)
    steps = [(across, step) for step in range(ring) for across in (1, 0) if across or step]
    steps.sort(key=lambda s: -min(s[1], ring - s[1]))
    peers = [lax.rem(side + across, 2) * ring + lax.rem(place_at + step, ring) for across, step in steps]
    with jax.named_scope("greet"):
        for peer in peers:
            pl.semaphore_signal(barrier, inc=1, device_id={"row": peer}, device_id_type=MESH)
        for partner in (up_to, low_to):
            pl.semaphore_signal(barrier, inc=1, device_id={"col": partner}, device_id_type=MESH)

    def send(at, source, target, peer):
        return pltpu.make_async_remote_copy(
            src_ref=source, dst_ref=target, send_sem=sum_send.at[at], recv_sem=sum_recv.at[at],
            device_id={"row": peer}, device_id_type=MESH,
        )

    def share(at):
        own = bands.at[at, row]
        for peer in peers:
            send(at, own, own, peer).start()

    def form(at, upper, lower):
        bands[at, row] = jnp.concatenate(gram_bands(upper, lower, place), axis=0)

    def summed(at):
        rest = bands.at[at, pl.ds(0, rows - 1)]
        with jax.named_scope("sum_wait"):
            send(at, rest, rest, peers[0]).wait_recv()
        whole = bands[at, 0]
        for d in range(1, rows):
            whole = whole + bands[at, d]
        total[at, 0:4 * KEPT] = whole
        return [unpack(total[at, KEPT * block:KEPT * block + ROWS]) for block in range(4)]

    total[...] = jnp.zeros(total.shape, F32)
    with jax.named_scope("load_slab"):
        load_s.wait()
    with jax.named_scope("gram_first"):
        form(0, s_own[:, :BLK], s_own[:, BLK:])
    with jax.named_scope("entry"):
        pl.semaphore_wait(barrier, rows + 1)
    share(0)

    def move(kind, at, source, target, pair, to):
        return pltpu.make_async_remote_copy(
            src_ref=source, dst_ref=target, send_sem=move_send.at[kind, at], recv_sem=move_recv.at[kind, pair],
            device_id={"col": to}, device_id_type=MESH,
        )

    s_moves = [
        move(0, at, s_own, s_other.at[pair], pair, to)
        for at, (pair, to) in enumerate(((up_pair, up_to), (low_pair, low_to)))
    ]
    for copy in s_moves:
        copy.start()
    blocks = summed(0)
    with jax.named_scope("solve_first"):
        parts = solve(*blocks)
        columns = [block_columns(parts, lower) for lower in (False, True)]
        for at, near in enumerate(columns):
            columns_own[at, :TALL], columns_own[at, TALL:] = near
    column_moves = [
        move(2, at, columns_own.at[at], columns_in.at[pair], pair, to)
        for at, (pair, to) in enumerate(((up_pair, up_to), (low_pair, low_to)))
    ]
    for copy in column_moves:
        copy.start()
    with jax.named_scope("rotation_first"):
        split = thirds(
            jnp.concatenate([whole_columns(near, lower) for near, lower in zip(columns, (False, True))], axis=1)
        )

    def rotate(own, half, parts):
        moved = times(halves(own[...]), parts)
        half[0] = moved[:, :BLK]
        half[1] = moved[:, BLK:]

    def stay(half, target):
        target[0, own_half[0]] = half[stays_a]
        target[1, own_half[1]] = half[stays_b]

    f_moves = [
        move(1, 0, f_half.at[0], f_pair.at[up_pair, up_half], up_pair, up_to),
        move(1, 1, f_half.at[1], f_pair.at[low_pair, low_half], low_pair, low_to),
    ]
    with jax.named_scope("apply_slab"):
        rotate(s_own, s_half, split)
        stay(s_half, s_pair)
    load_f.wait()
    with jax.named_scope("apply_factor"):
        rotate(f_own, f_half, split[:2])
        stay(f_half, f_pair)

    def arrived(kind, target, pair):
        move(kind, 0, target, target, pair, up_to).wait_recv()

    def keep_halves(whole, pair, split):
        split[0, pair], split[1, pair] = halves(whole)

    def pick(choices, at):
        return jnp.where(at == 0, choices[0], choices[1])

    first = jnp.where((col >= pairs // 2) & (col < pairs // 2 + 4), 1, 0)
    order = (first, 1 - first)
    for pair in order:
        with jax.named_scope("slab_arrival"):
            arrived(0, s_other.at[pair], pair)
        with jax.named_scope("split_other"):
            keep_halves(s_other[pair], pair, s_split)
        with jax.named_scope("columns_arrival"):
            arrived(2, columns_in.at[pair], pair)
        with jax.named_scope("rotation_other"):
            near = [columns_in[pair, :TALL], columns_in[pair, TALL:]]
            rotation = thirds(whole_columns(near, pick(other_lower, pair)))
        with jax.named_scope("apply_other"):
            s_pair[pair, 1 - pick(own_half, pair)] = times((s_split[0, pair], s_split[1, pair]), rotation)
        with jax.named_scope("gram_second"):
            form(1 + pair, s_pair[pair, 0], s_pair[pair, 1])
        share(1 + pair)
    for copy in f_moves:
        copy.start()

    lower_of = (col == 1, col != last)

    def joined(target, pair):
        return jnp.concatenate([target[pair, 0], target[pair, 1]], axis=1)

    def finish(split, done, pair, rotation):
        at = pl.ds(pl.multiple_of(pair * BLK, BLK), BLK)
        done[:, at] = times((split[0, pair], split[1, pair]), rotation)

    with jax.named_scope("split_slab"):
        for pair in range(2):
            keep_halves(joined(s_pair, pair), pair, s_split)
    for pair in order:
        blocks = summed(1 + pair)
        with jax.named_scope("solve_second"):
            parts = solve(*blocks)
        with jax.named_scope("rotation_second"):
            lower = pick(lower_of, pair)
            rotation = halves(whole_columns(block_columns(parts, lower), lower))
        with jax.named_scope("finish_slab"):
            finish(s_split, s_done, pair, rotation)
        with jax.named_scope("factor_arrival"):
            arrived(1, f_half.at[0], pair)
        with jax.named_scope("split_factor"):
            keep_halves(joined(f_pair, pair), pair, f_split)
        with jax.named_scope("finish_factor"):
            finish(f_split, f_done, pair, rotation)
    store_s = pltpu.make_async_copy(s_done, s_out, store_sem.at[0])
    store_f = pltpu.make_async_copy(f_done, f_out, store_sem.at[1])
    store_s.start()
    store_f.start()

    with jax.named_scope("last_waits"):
        for copy in s_moves + column_moves + f_moves:
            copy.wait_send()
        for at in range(3):
            rest = bands.at[at, pl.ds(0, rows - 1)]
            send(at, rest, rest, peers[0]).wait_send()
        store_s.wait()
        store_f.wait()


def store(s_done, f_done, s_out, f_out, sem):
    copies = [
        pltpu.make_async_copy(source, target, sem.at[at])
        for at, (source, target) in enumerate(((s_done, s_out), (f_done, f_out)))
    ]
    for copy in copies:
        copy.start()
    for copy in copies:
        copy.wait()


def solution(mesh):
    rows, pairs = mesh.shape["row"], mesh.shape["col"]

    def shards(matrix, right_factor):
        s_rows, f_rows = matrix.shape[0], right_factor.shape[0]
        done = pl.pallas_call(
            lambda *refs: kernel(rows, pairs, *refs),
            out_shape=(
                pltpu.VMEM(matrix.shape, F32),
                pltpu.VMEM(right_factor.shape, F32),
            ),
            in_specs=[pl.BlockSpec(memory_space=pl.ANY)] * 2,
            out_specs=[pl.BlockSpec(memory_space=pl.ANY)] * 2,
            scratch_shapes=[
                pltpu.VMEM(matrix.shape, F32),
                pltpu.VMEM(right_factor.shape, F32),
                pltpu.VMEM((2, s_rows, BLK), F32),
                pltpu.VMEM((2, f_rows, BLK), F32),
                pltpu.VMEM((2, 2, s_rows, BLK), F32),
                pltpu.VMEM((2, 2, f_rows, BLK), F32),
                pltpu.VMEM((2, 2, s_rows, 2 * BLK), jnp.bfloat16),
                pltpu.VMEM((2, 2, f_rows, 2 * BLK), jnp.bfloat16),
                pltpu.VMEM(matrix.shape, F32),
                pltpu.VMEM(right_factor.shape, F32),
                pltpu.VMEM((3, rows, 4 * KEPT, BLK), F32),
                pltpu.VMEM((4 * TALL + ROWS, BLK), F32),
                pltpu.VMEM((3, 4 * ROWS, BLK), F32),
                pltpu.VMEM((2,) + matrix.shape, F32),
                pltpu.VMEM((2, 2 * TALL, BLK), F32),
                pltpu.VMEM((2, 2 * TALL, BLK), F32),
                pltpu.SemaphoreType.DMA((2,)),
                pltpu.SemaphoreType.DMA((2,)),
                pltpu.SemaphoreType.DMA((3,)),
                pltpu.SemaphoreType.DMA((3,)),
                pltpu.SemaphoreType.DMA((3, 2)),
                pltpu.SemaphoreType.DMA((3, 2)),
            ],
            compiler_params=pltpu.CompilerParams(collective_id=0, has_side_effects=True, vmem_limit_bytes=GRANT),
            name="tournament",
        )(*[pltpu.with_memory_space_constraint(x, pltpu.HBM) for x in (matrix, right_factor)])
        return pl.pallas_call(
            store,
            out_shape=(pltpu.HBM(matrix.shape, F32), pltpu.HBM(right_factor.shape, F32)),
            in_specs=[pl.BlockSpec(memory_space=pl.ANY)] * 2,
            out_specs=[pl.BlockSpec(memory_space=pl.ANY)] * 2,
            scratch_shapes=[pltpu.SemaphoreType.DMA((2,))],
            compiler_params=pltpu.CompilerParams(vmem_limit_bytes=GRANT),
            name="store",
        )(*[pltpu.with_memory_space_constraint(x, pltpu.VMEM) for x in done])

    spec = P("row", "col")
    return jax.shard_map(shards, mesh=mesh, in_specs=(spec, spec), out_specs=(spec, spec), check_vma=False)
```

```python
import jax
import jax.numpy as jnp
from jax import lax
from jax.experimental import pallas as pl
from jax.experimental.pallas import tpu as pltpu
from jax.sharding import PartitionSpec as P

BLK = 128
ROUNDS = 6
ROWS = 8
TALL = 16
KEPT = 6
GRANT = 32 * 1024 * 1024
MESH = pl.DeviceIdType.MESH
F32 = jnp.float32


def iota(shape, axis):
    return lax.broadcasted_iota(jnp.int32, shape, axis)


def next_lane(x):
    return pltpu.roll(x, BLK - 1, 1)


def previous_lane(x):
    return pltpu.roll(x, 1, 1)


def below(x, n):
    even, odd = x
    up_even, up_odd = pltpu.roll(even, ROWS - 1, 0), pltpu.roll(odd, ROWS - 1, 0)
    return (odd, up_even) if n == 1 else (up_even, up_odd)


def above(x, n):
    even, odd = x
    down_even, down_odd = pltpu.roll(even, 1, 0), pltpu.roll(odd, 1, 0)
    return (down_odd, even) if n == 1 else (down_even, down_odd)


def both(function, *operands):
    return tuple(function(*parts) for parts in zip(*operands))


def lanes(x, index):
    return jnp.take_along_axis(x, jnp.broadcast_to(index, x.shape), axis=1)


def halves(x):
    high = x.astype(jnp.bfloat16)
    return high, (x - high.astype(F32)).astype(jnp.bfloat16)


def dot(x, y):
    return jnp.dot(x, y, preferred_element_type=F32)


def thirds(x):
    high, rest = halves(x)
    return high, rest, (x - high.astype(F32) - rest.astype(F32)).astype(jnp.bfloat16)


def times(x_split, split):
    x_high, x_low = x_split
    high, low = split[:2]
    width = high.shape[1]
    if width == BLK:
        beside = jnp.concatenate([high, low], axis=1)
        first, second = dot(x_high, beside), dot(x_low, beside)
        small = first[:, width:] + (second[:, :width] + second[:, width:])
        large = first[:, :width]
    else:
        small = dot(x_low, high) + dot(x_high, low)
        large = dot(x_high, high)
    if len(split) == 3:
        small = small + dot(x_high, split[2])
    return large + small


def products(x, y):
    x_parts, y_parts = thirds(x.T), thirds(y)
    count = x.shape[1]
    by_high = dot(jnp.concatenate(x_parts, axis=0), y_parts[0])
    by_middle = dot(jnp.concatenate(x_parts[:2], axis=0), y_parts[1])
    smallest = by_high[2 * count:] + by_middle[count:] + dot(x_parts[0], y_parts[2])
    return by_high[:count] + ((by_high[count:2 * count] + by_middle[:count]) + smallest)


def backwards(x):
    return lanes(x, BLK - 1 - iota((1, BLK), 1))


def diagonals(blocks, place):
    lane = iota((BLK, BLK), 1)
    beside = pltpu.roll(blocks[0], 1, 1, stride=1, stride_axis=0)
    for at, block in enumerate(blocks[1:], 1):
        turned = pltpu.roll(block, 1 + at * TALL, 1, stride=1, stride_axis=0)
        beside = jnp.where(lane >= at * TALL, turned, beside)
    place[:len(blocks) * TALL] = beside.T[:len(blocks) * TALL]
    return [
        tuple(place[pl.ds(at * TALL + odd, ROWS, stride=2)] for odd in range(2)) for at in range(len(blocks))
    ]


def flipped_rows(x):
    index = jnp.clip(KEPT - 1 - iota(x.shape, 0), 0, ROWS - 1)
    return jnp.take_along_axis(x, index, axis=0)


def pack(even, odd):
    j, lane = iota((ROWS, BLK), 0), iota((ROWS, BLK), 1)
    odd = flipped_rows(odd)
    high = pltpu.roll(odd, 0, 1, stride=1, stride_axis=0)
    low = pltpu.roll(pltpu.roll(odd, 0, 1, stride=3, stride_axis=0), BLK - 11, 1)
    return jnp.where(lane < j, high, jnp.where(lane < 2 * j, low, even))[:KEPT]


def unpack(packed):
    i, lane = iota((ROWS, BLK), 0), iota((ROWS, BLK), 1)
    back = flipped_rows(packed)
    high = pltpu.roll(pltpu.roll(back, 0, 1, stride=1, stride_axis=0), BLK - 5, 1)
    low = pltpu.roll(pltpu.roll(back, 0, 1, stride=3, stride_axis=0), BLK - 4, 1)
    return packed, jnp.where(lane >= BLK - 5 + i, high, low)


def gram_bands(upper, lower, place):
    left = jnp.concatenate([upper, backwards(lower)], axis=1)
    right = jnp.concatenate([backwards(upper), lower], axis=1)
    gram = products(left, right)
    blocks = (gram[:BLK, :BLK], gram[:BLK, BLK:], gram[BLK:, :BLK], gram[BLK:, BLK:])
    return [pack(*pair) for pair in diagonals(blocks, place)]


def angles(round_index, uu, uv, vv):
    lane = iota((1, BLK), 1)
    spread = vv[0][0:1] - uu[0][0:1]
    across = 2.0 * uv[0][0:1]
    width = jnp.abs(spread)
    scale = jnp.where(jnp.maximum(jnp.abs(across), width) < 1e-12, 1e20, 1.0)
    across = across * scale
    width = width * scale
    norm = across * across + width * width
    root = jnp.where(norm > 0, lax.rsqrt(norm), 0.0)
    square = jnp.where(norm > 0, 0.5 + 0.5 * width * root, 1.0)
    root_cosine = lax.rsqrt(square)
    cosine = square * root_cosine
    sine = 0.5 * across * root * root_cosine
    upper_first = (lane == 0) | (lane > round_index)
    positive = (spread > 0) | ((spread == 0) & upper_first)
    return cosine, jnp.where(positive, sine, -sine)


def shift_pairs(uu, uv, vu, vv):
    lane, row = iota((ROWS, BLK), 1), iota((ROWS, BLK), 0)
    last, first, second = lane == BLK - 1, lane == 0, lane == 1
    uu_next, uv_next = both(next_lane, uu), both(next_lane, uv)
    uu_back, uv_back, vu_back, vv_back = (both(previous_lane, x) for x in (uu, uv, vu, vv))
    vu_1, vv_b1, uv_n1 = above(vu, 1), below(vv, 1), below(uv_next, 1)
    uu_n2, uv_n2, vu_b2, vv_b1up = below(uu_next, 2), below(uv_next, 2), above(vu_back, 2), above(vv_back, 1)
    uv_b1up = above(uv_back, 1)
    out = []
    for at in range(2):
        q = 2 * row + at
        new_uu = jnp.where(last, vu_1[at] if at else jnp.where(q == 0, vv[at], vu_1[at]), uu_next[at])
        new_uv = jnp.where(q == lane - 1, uu_n2[at], uv_n2[at])
        new_uv = jnp.where(q == lane, uv_n1[at], new_uv)
        new_uv = jnp.where(last, vv_b1[at], new_uv)
        if at:
            new_vu = jnp.where(q == 1, jnp.where(second, uu[at], uv[at]), vu_b2[at])
        else:
            new_vu = jnp.where(q == 0, new_uv, vu_b2[at])
        new_vv = jnp.where(q == lane - 1, vu_back[at], vv_back[at])
        new_vv = jnp.where(q == lane, vv_b1up[at], new_vv)
        new_vv = jnp.where(first, vv[at], new_vv)
        new_vv = jnp.where(second & (q == at), uv_b1up[at] if at else uu_back[at], new_vv)
        out.append((new_uu, new_uv, new_vu, new_vv))
    return tuple(zip(*out))


def turn_columns(part, cos, sin):
    to_u, to_v = part
    return to_u * cos - to_v * sin, to_u * sin + to_v * cos


def shift_columns(part):
    to_u, to_v = part
    lane = iota((TALL, BLK), 1)
    moved_u = pltpu.roll(next_lane(to_u), 1, 0)
    moved_v = pltpu.roll(jnp.where(lane == 1, previous_lane(to_u), previous_lane(to_v)), TALL - 1, 0)
    return jnp.where(lane == BLK - 1, to_v, moved_u), jnp.where(lane == 0, to_v, moved_v)


def solve(uu, uv, vu, vv):
    one = jnp.where(iota((TALL, BLK), 0) == ROWS, 1.0, 0.0).astype(F32)
    none = jnp.zeros((TALL, BLK), F32)
    parts = ((one, none), (none, one))

    def turn(round_index, state):
        (uu, uv, vu, vv), parts = state
        cos, sin = angles(round_index, uu, uv, vv)
        parts = tuple(turn_columns(part, cos, sin) for part in parts)
        near = [jnp.broadcast_to(x, (ROWS, BLK)) for x in (cos, sin)]
        new = []
        for at in range(2):
            far_cos, far_sin = (pltpu.roll(x, at, 1, stride=2, stride_axis=0) for x in near)
            a, b, c, d = uu[at], uv[at], vu[at], vv[at]
            a, b = a * far_cos - b * far_sin, a * far_sin + b * far_cos
            c, d = c * far_cos - d * far_sin, c * far_sin + d * far_cos
            a, c = a * cos - c * sin, a * sin + c * cos
            b, d = b * cos - d * sin, b * sin + d * cos
            new.append((a, b, c, d))
        return shift_pairs(*zip(*new)), tuple(shift_columns(part) for part in parts)

    blocks, parts = lax.fori_loop(0, ROUNDS - 1, turn, ((uu, uv, vu, vv), parts))
    cos, sin = angles(ROUNDS - 1, blocks[0], blocks[1], blocks[3])
    return [turn_columns(part, cos, sin) for part in parts]


def column_places(lower):
    last_round = ROUNDS - 1
    lane = iota((1, BLK), 1)
    upper_place = jnp.where(lane >= last_round, lane - last_round, last_round - lane)
    from_u = BLK - last_round + lane
    from_v = jnp.where(lane == BLK - 1, 0, BLK - 1 + last_round - lane)
    place = jnp.where(lower, jnp.where(lane < last_round, from_u, from_v), upper_place)
    first = lane < last_round
    in_u = (first & lower) | (jnp.logical_not(first) & jnp.logical_not(lower))
    return in_u, place


def block_columns(parts, lower):
    in_u, place = column_places(lower)
    return [jnp.where(in_u, lanes(to_u, place), lanes(to_v, place)) for to_u, to_v in parts]


def spread_rows(near, start):
    tall = jnp.concatenate([near, jnp.zeros((ROWS, BLK), F32)], axis=0)
    for bit in (1, 2, 4):
        tall = jnp.where((start & bit) != 0, pltpu.roll(tall, bit, 0), tall)
    tile = start >> 3
    out = []
    for at in range(BLK // ROWS):
        rows = jnp.where(tile == at - 1, tall[2 * ROWS:], 0.0)
        rows = jnp.where(tile == at, tall[ROWS:2 * ROWS], rows)
        out.append(jnp.where(tile == at + 1, tall[:ROWS], rows))
    return out


def whole_columns(near, lower):
    place = column_places(lower)[1]
    from_u, from_v = near
    flip = ROWS - 1 - iota((ROWS, BLK), 0)
    from_v = [jnp.take_along_axis(x, flip, axis=0) for x in (from_v[ROWS:], from_v[:ROWS])]
    tiles = spread_rows(from_u, place) + spread_rows(jnp.concatenate(from_v, axis=0), BLK - place)
    return jnp.concatenate(tiles, axis=0)


def kernel(
    rows, pairs,
    s_in, f_in, s_out, f_out,
    s_own, f_own, s_half, f_half, s_pair, f_pair, s_split, f_split, s_done, f_done, bands, place,
    s_other, columns_own, columns_in,
    load_sem, store_sem, sum_send, sum_recv, move_send, move_recv,
):
    load_s = pltpu.make_async_copy(s_in, s_own, load_sem.at[0])
    load_f = pltpu.make_async_copy(f_in, f_own, load_sem.at[1])
    with jax.named_scope("loads"):
        load_s.start()
        load_f.start()
    row, col = lax.axis_index("row"), lax.axis_index("col")
    last = pairs - 1

    up_to = jnp.where(col == 0, 1, jnp.where(col == last, last - 1, jnp.where(col == last - 1, last, col + 2)))
    up_pair = jnp.where(col >= last - 1, 1, 0)
    up_half = jnp.where(col == last, 1, 0)
    low_to = jnp.where(col == 0, 2, jnp.where(col == 1, 0, col - 2))
    low_pair = jnp.where(col <= 1, 0, 1)
    low_half = jnp.where(col == 0, 0, 1)
    stays_a = jnp.where(col == 0, 0, 1)
    stays_b = jnp.where(col == 0, 1, 0)
    own_half = (stays_a, jnp.where(col == last, 1, 0))
    other_lower = ((col == 0) | (col == 2), col < last - 1)

    barrier = pltpu.get_barrier_semaphore()
    ring = rows // 2
    side, place_at = row // ring, lax.rem(row, ring)
    steps = [(across, step) for step in range(ring) for across in (1, 0) if across or step]
    steps.sort(key=lambda s: -min(s[1], ring - s[1]))
    peers = [lax.rem(side + across, 2) * ring + lax.rem(place_at + step, ring) for across, step in steps]
    with jax.named_scope("greet"):
        for peer in peers:
            pl.semaphore_signal(barrier, inc=1, device_id={"row": peer}, device_id_type=MESH)
        for partner in (up_to, low_to):
            pl.semaphore_signal(barrier, inc=1, device_id={"col": partner}, device_id_type=MESH)

    def send(at, source, target, peer):
        return pltpu.make_async_remote_copy(
            src_ref=source, dst_ref=target, send_sem=sum_send.at[at], recv_sem=sum_recv.at[at],
            device_id={"row": peer}, device_id_type=MESH,
        )

    def share(at):
        own = bands.at[at, row]
        for peer in peers:
            send(at, own, own, peer).start()

    def form(at, upper, lower):
        bands[at, row] = jnp.concatenate(gram_bands(upper, lower, place), axis=0)

    def summed(at):
        rest = bands.at[at, pl.ds(0, rows - 1)]
        with jax.named_scope("sum_wait"):
            send(at, rest, rest, peers[0]).wait_recv()
        whole = bands[at, 0]
        for d in range(1, rows):
            whole = whole + bands[at, d]
        whole = jnp.concatenate([whole, jnp.zeros((ROWS, BLK), F32)], axis=0)
        return [unpack(whole[KEPT * block:KEPT * block + ROWS]) for block in range(4)]

    with jax.named_scope("load_slab"):
        load_s.wait()
    with jax.named_scope("gram_first"):
        form(0, s_own[:, :BLK], s_own[:, BLK:])
    with jax.named_scope("entry"):
        pl.semaphore_wait(barrier, rows + 1)
    share(0)

    def move(kind, at, source, target, pair, to):
        return pltpu.make_async_remote_copy(
            src_ref=source, dst_ref=target, send_sem=move_send.at[kind, at], recv_sem=move_recv.at[kind, pair],
            device_id={"col": to}, device_id_type=MESH,
        )

    s_moves = [
        move(0, at, s_own, s_other.at[pair], pair, to)
        for at, (pair, to) in enumerate(((up_pair, up_to), (low_pair, low_to)))
    ]
    for copy in s_moves:
        copy.start()
    blocks = summed(0)
    with jax.named_scope("solve_first"):
        parts = solve(*blocks)
        columns = [block_columns(parts, lower) for lower in (False, True)]
        for at, near in enumerate(columns):
            columns_own[at, :TALL], columns_own[at, TALL:] = near
    column_moves = [
        move(2, at, columns_own.at[at], columns_in.at[pair], pair, to)
        for at, (pair, to) in enumerate(((up_pair, up_to), (low_pair, low_to)))
    ]
    for copy in column_moves:
        copy.start()
    with jax.named_scope("rotation_first"):
        split = thirds(
            jnp.concatenate([whole_columns(near, lower) for near, lower in zip(columns, (False, True))], axis=1)
        )

    def rotate(own, half, parts):
        moved = times(halves(own[...]), parts)
        half[0] = moved[:, :BLK]
        half[1] = moved[:, BLK:]

    def stay(half, target):
        target[0, own_half[0]] = half[stays_a]
        target[1, own_half[1]] = half[stays_b]

    f_moves = [
        move(1, 0, f_half.at[0], f_pair.at[up_pair, up_half], up_pair, up_to),
        move(1, 1, f_half.at[1], f_pair.at[low_pair, low_half], low_pair, low_to),
    ]
    with jax.named_scope("apply_slab"):
        rotate(s_own, s_half, split)
        stay(s_half, s_pair)
    load_f.wait()
    with jax.named_scope("apply_factor"):
        rotate(f_own, f_half, split[:2])
        stay(f_half, f_pair)

    def arrived(kind, target, pair):
        move(kind, 0, target, target, pair, up_to).wait_recv()

    def keep_halves(whole, pair, split):
        split[0, pair], split[1, pair] = halves(whole)

    def pick(choices, at):
        return jnp.where(at == 0, choices[0], choices[1])

    first = jnp.where((col >= pairs // 2) & (col < pairs // 2 + 4), 1, 0)
    order = (first, 1 - first)
    for pair in order:
        with jax.named_scope("slab_arrival"):
            arrived(0, s_other.at[pair], pair)
        with jax.named_scope("split_other"):
            keep_halves(s_other[pair], pair, s_split)
        with jax.named_scope("columns_arrival"):
            arrived(2, columns_in.at[pair], pair)
        with jax.named_scope("rotation_other"):
            near = [columns_in[pair, :TALL], columns_in[pair, TALL:]]
            rotation = thirds(whole_columns(near, pick(other_lower, pair)))
        with jax.named_scope("apply_other"):
            s_pair[pair, 1 - pick(own_half, pair)] = times((s_split[0, pair], s_split[1, pair]), rotation)
        with jax.named_scope("gram_second"):
            form(1 + pair, s_pair[pair, 0], s_pair[pair, 1])
        share(1 + pair)
    for copy in f_moves:
        copy.start()

    lower_of = (col == 1, col != last)

    def joined(target, pair):
        return jnp.concatenate([target[pair, 0], target[pair, 1]], axis=1)

    def finish(split, done, pair, rotation):
        at = pl.ds(pl.multiple_of(pair * BLK, BLK), BLK)
        done[:, at] = times((split[0, pair], split[1, pair]), rotation)

    with jax.named_scope("split_slab"):
        for pair in range(2):
            keep_halves(joined(s_pair, pair), pair, s_split)
    for step, pair in enumerate(order):
        blocks = summed(1 + pair)
        with jax.named_scope("solve_second"):
            parts = solve(*blocks)
        with jax.named_scope("rotation_second"):
            lower = pick(lower_of, pair)
            rotation = halves(whole_columns(block_columns(parts, lower), lower))
        if step == 0:
            with jax.named_scope("finish_slab"):
                finish(s_split, s_done, pair, rotation)
        with jax.named_scope("factor_arrival"):
            arrived(1, f_half.at[0], pair)
        with jax.named_scope("split_factor"):
            keep_halves(joined(f_pair, pair), pair, f_split)
        with jax.named_scope("finish_factor"):
            if step == 0:
                finish(f_split, f_done, pair, rotation)
            else:
                stacked = [jnp.concatenate([s_split[i, pair], f_split[i, pair]], axis=0) for i in range(2)]
                result = times(stacked, rotation)
                at = pl.ds(pl.multiple_of(pair * BLK, BLK), BLK)
                s_done[:, at] = result[:s_done.shape[0]]
                f_done[:, at] = result[s_done.shape[0]:]
    store_s = pltpu.make_async_copy(s_done, s_out, store_sem.at[0])
    store_f = pltpu.make_async_copy(f_done, f_out, store_sem.at[1])
    store_s.start()
    store_f.start()

    with jax.named_scope("last_waits"):
        for copy in s_moves + column_moves + f_moves:
            copy.wait_send()
        for at in range(3):
            rest = bands.at[at, pl.ds(0, rows - 1)]
            send(at, rest, rest, peers[0]).wait_send()
        store_s.wait()
        store_f.wait()


def store(s_done, f_done, s_out, f_out, sem):
    copies = [
        pltpu.make_async_copy(source, target, sem.at[at])
        for at, (source, target) in enumerate(((s_done, s_out), (f_done, f_out)))
    ]
    for copy in copies:
        copy.start()
    for copy in copies:
        copy.wait()


def solution(mesh):
    rows, pairs = mesh.shape["row"], mesh.shape["col"]

    def shards(matrix, right_factor):
        s_rows, f_rows = matrix.shape[0], right_factor.shape[0]
        done = pl.pallas_call(
            lambda *refs: kernel(rows, pairs, *refs),
            out_shape=(
                pltpu.VMEM(matrix.shape, F32),
                pltpu.VMEM(right_factor.shape, F32),
            ),
            in_specs=[pl.BlockSpec(memory_space=pl.ANY)] * 2,
            out_specs=[pl.BlockSpec(memory_space=pl.ANY)] * 2,
            scratch_shapes=[
                pltpu.VMEM(matrix.shape, F32),
                pltpu.VMEM(right_factor.shape, F32),
                pltpu.VMEM((2, s_rows, BLK), F32),
                pltpu.VMEM((2, f_rows, BLK), F32),
                pltpu.VMEM((2, 2, s_rows, BLK), F32),
                pltpu.VMEM((2, 2, f_rows, BLK), F32),
                pltpu.VMEM((2, 2, s_rows, 2 * BLK), jnp.bfloat16),
                pltpu.VMEM((2, 2, f_rows, 2 * BLK), jnp.bfloat16),
                pltpu.VMEM(matrix.shape, F32),
                pltpu.VMEM(right_factor.shape, F32),
                pltpu.VMEM((3, rows, 4 * KEPT, BLK), F32),
                pltpu.VMEM((4 * TALL + ROWS, BLK), F32),
                pltpu.VMEM((2,) + matrix.shape, F32),
                pltpu.VMEM((2, 2 * TALL, BLK), F32),
                pltpu.VMEM((2, 2 * TALL, BLK), F32),
                pltpu.SemaphoreType.DMA((2,)),
                pltpu.SemaphoreType.DMA((2,)),
                pltpu.SemaphoreType.DMA((3,)),
                pltpu.SemaphoreType.DMA((3,)),
                pltpu.SemaphoreType.DMA((3, 2)),
                pltpu.SemaphoreType.DMA((3, 2)),
            ],
            compiler_params=pltpu.CompilerParams(collective_id=0, has_side_effects=True, vmem_limit_bytes=GRANT),
            name="tournament",
        )(*[pltpu.with_memory_space_constraint(x, pltpu.HBM) for x in (matrix, right_factor)])
        return pl.pallas_call(
            store,
            out_shape=(pltpu.HBM(matrix.shape, F32), pltpu.HBM(right_factor.shape, F32)),
            in_specs=[pl.BlockSpec(memory_space=pl.ANY)] * 2,
            out_specs=[pl.BlockSpec(memory_space=pl.ANY)] * 2,
            scratch_shapes=[pltpu.SemaphoreType.DMA((2,))],
            compiler_params=pltpu.CompilerParams(vmem_limit_bytes=GRANT),
            name="store",
        )(*[pltpu.with_memory_space_constraint(x, pltpu.VMEM) for x in done])

    spec = P("row", "col")
    return jax.shard_map(shards, mesh=mesh, in_specs=(spec, spec), out_specs=(spec, spec), check_vma=False)
```
